32 devices in a mesh: ctx: 8 (over z, x), fsdp: 4 (over y, core).
Axes of the slice: x: 2, y: 2, z: 4, core: 2. Of those that a mesh axis runs over, the one named last changes fastest.
Arguments:
- tokens: bfloat16 [4, 1024, 2048], P('fsdp', 'ctx'), may hold values from -7 to 7
- cotangent: bfloat16 [4, 1024, 2048], P('fsdp', 'ctx'), may hold values from -7 to 7
- positions: int32 [4, 1024], P('fsdp'), may hold values from 0 to 1023, as said below
- segments: int32 [4, 1024], P('fsdp'), may hold values from 0 to 3, as said below
- joint_weight: float32 [2048, 6144], P(('ctx', 'fsdp')), may hold values from -0.125 to 0.125
- joint_mean: float32 [2048, 6144], P(('ctx', 'fsdp')), may hold values from -0.00012207031 to 0.00012207031
- joint_square: float32 [2048, 6144], P(('ctx', 'fsdp')), may hold values from 1.5497208e-09 to 6.1392784e-09
- output_weight: float32 [2048, 2048], P(('ctx', 'fsdp')), may hold values from -1.5 to 1.5
- output_mean: float32 [2048, 2048], P(('ctx', 'fsdp')), may hold values from -1.5258789e-05 to 1.5258789e-05
- output_square: float32 [2048, 2048], P(('ctx', 'fsdp')), may hold values from 3.1590463e-11 to 1.2516975e-10
- expand_weight: float32 [2048, 16384], P(('ctx', 'fsdp')), may hold values from -0.125 to 0.125
- expand_mean: float32 [2048, 16384], P(('ctx', 'fsdp')), may hold values from -5.340576e-05 to 5.340576e-05
- expand_square: float32 [2048, 16384], P(('ctx', 'fsdp')), may hold values from 3.3974648e-10 to 1.3709068e-09
- shrink_weight: float32 [2048, 8192], P(('ctx', 'fsdp')), may hold values from -0.0625 to 0.0625
- shrink_mean: float32 [2048, 8192], P(('ctx', 'fsdp')), may hold values from -0.00010681152 to 0.00010681152
- shrink_square: float32 [2048, 8192], P(('ctx', 'fsdp')), may hold values from 1.3113022e-09 to 5.3048135e-09
Outputs:
- layer_output: bfloat16 [4, 1024, 2048], P('fsdp', 'ctx')
- input_grad: float32 [4, 1024, 2048], P('fsdp', 'ctx')
- grad_norm: float32 [], replicated
- joint_next: float32 [2048, 6144], P(('ctx', 'fsdp'))
- joint_mean_next: float32 [2048, 6144], P(('ctx', 'fsdp'))
- joint_square_next: float32 [2048, 6144], P(('ctx', 'fsdp'))
- output_next: float32 [2048, 2048], P(('ctx', 'fsdp'))
- output_mean_next: float32 [2048, 2048], P(('ctx', 'fsdp'))
- output_square_next: float32 [2048, 2048], P(('ctx', 'fsdp'))
- expand_next: float32 [2048, 16384], P(('ctx', 'fsdp'))
- expand_mean_next: float32 [2048, 16384], P(('ctx', 'fsdp'))
- expand_square_next: float32 [2048, 16384], P(('ctx', 'fsdp'))
- shrink_next: float32 [2048, 8192], P(('ctx', 'fsdp'))
- shrink_mean_next: float32 [2048, 8192], P(('ctx', 'fsdp'))
- shrink_square_next: float32 [2048, 8192], P(('ctx', 'fsdp'))
The draws below stay inside these ranges and needn't reach their ends.
Inputs may be any that keep to these rules, and one draw needn't show every extreme that they name: Within a sequence the 128 tokens of one device along ctx hold the positions b * 64 to b * 64 + 63 and then (15 - b) * 64 to (15 - b) * 64 + 63, each run ascending, with a different b on each device. `segments`: each sequence holds exactly four documents, numbered 0 to 3 in the order of their positions; one of them holds half of the 1024 positions or more and contains the first or the last position.
All inputs are finite; a program needn't handle non-finite values.
Results may differ from the reference program's by a relative error of at most 0.02.
Values may be sent and summed in bfloat16 or wider, within the bound.
No kernel may reach another device: no remote copies, remote signals or barrier semaphores. Data moves between devices by JAX's collectives and lax.ppermute only.
A program may use at most 896 MiB of HBM per device.

```python
import math
import jax
import jax.numpy as jnp
from jax import lax

D = 2048
HEAD_DIM = 128
FF = 8192
TOK_DEV = 128
STEP = 10
RANKS = 8
SEQUENCES = 4
LENGTH = 1024
HALF = 64


def column_ramp(growth):
    shard_count = RANKS * SEQUENCES
    column = jnp.arange(D) // (D // shard_count)
    outer_part = (column // SEQUENCES).astype(jnp.float32) / max(RANKS - 1, 1)
    inner_part = (column % SEQUENCES).astype(jnp.float32) / max(SEQUENCES - 1, 1)
    return growth ** ((outer_part + inner_part) * 0.5 - 0.5)


def draw_tokens(key, part):
    key = jax.random.fold_in(key, 11)
    samples = jnp.clip(jax.random.normal(key, (SEQUENCES, LENGTH, D), jnp.float32), -4.0, 4.0)
    return (samples * column_ramp(3.0)).astype(jnp.bfloat16)


def draw_cotangent(key, part):
    key = jax.random.fold_in(key, 12)
    samples = jnp.clip(jax.random.normal(key, (SEQUENCES, LENGTH, D), jnp.float32), -4.0, 4.0)
    return (samples * column_ramp(3.0)).astype(jnp.bfloat16)


def document_layout(key):
    places = jnp.arange(LENGTH)
    device_slot = places // TOK_DEV
    within = places % TOK_DEV

    def one_sequence(sequence_key):
        block_order = jax.random.permutation(jax.random.fold_in(sequence_key, 1), RANKS)
        chosen = block_order[device_slot]
        lower_half = within < HALF
        position = jnp.where(lower_half, chosen * HALF + within, (2 * RANKS - 1 - chosen) * HALF + within - HALF)
        long_side = jax.random.randint(jax.random.fold_in(sequence_key, 2), (), 0, 2)
        longest = LENGTH // 2 + jax.random.randint(jax.random.fold_in(sequence_key, 3), (), 0, LENGTH // 4 + 1)
        short_size = LENGTH - longest
        short_start = jnp.where(long_side == 0, longest, 0)
        first_cut = short_start + 1 + jax.random.randint(jax.random.fold_in(sequence_key, 4), (), 0, short_size // 2 - 1)
        second_cut = first_cut + 1 + jax.random.randint(jax.random.fold_in(sequence_key, 5), (), 0, short_size // 2 - 1)
        border = jnp.where(long_side == 0, longest, short_size)
        starts = (places == 0) | (places == border) | (places == first_cut) | (places == second_cut)
        document = jnp.cumsum(starts.astype(jnp.int32)) - 1
        return (position.astype(jnp.int32), document[position].astype(jnp.int32))
    return jax.vmap(one_sequence)(jax.random.split(key, SEQUENCES))


def draw_positions(key, part):
    return document_layout(key)[0]


def draw_segments(key, part):
    return document_layout(key)[1]


def block_scale(rng, dims, cuts, smallest, largest):
    factor_of, own = 1.0, jax.random.fold_in(rng, 6)
    for dim, blocks in cuts:
        draws = jnp.exp(jax.random.uniform(jax.random.fold_in(own, dim), (blocks,), jnp.float32, smallest / len(cuts), largest / len(cuts)))
        factor_of = factor_of * jnp.repeat(draws, dims[dim] // blocks).reshape([-1 if axis == dim else 1 for axis in range(len(dims))])
    return factor_of


def noise(rng, dims, spread, reach, shards=(), kind=jnp.bfloat16):
    gain = block_scale(rng, dims, shards, -0.22, 0.18) if shards else 1.0
    values = jax.random.normal(rng, dims, jnp.float32) * spread * gain
    return jnp.minimum(jnp.maximum(values, -reach), reach).astype(kind)


def setup_inputs(seed: int = 0) -> dict:
    seeds = jax.random.split(jax.random.key(seed), 17)
    tokens = draw_tokens(jax.random.fold_in(seeds[16], 71), 0)
    cotangent = draw_cotangent(jax.random.fold_in(seeds[16], 71), 0)
    positions = draw_positions(jax.random.fold_in(seeds[16], 71), 0)
    segments = draw_segments(jax.random.fold_in(seeds[16], 71), 0)
    joint_weight = noise(seeds[4], (D, 3 * D), D ** -0.5, 0.125, ((0, 32),), jnp.float32)
    joint_mean = noise(seeds[5], (D, 3 * D), (0.078 / (D * FF) ** 0.5), 0.00012207031, ((0, 32),), jnp.float32)
    joint_square = jnp.clip(jnp.exp(math.log(6.139278418970662e-09) - 1.3766324 * jax.random.uniform(seeds[6], (D, 3 * D), jnp.float32) ** block_scale(seeds[6], (D, 3 * D), ((0, 32),), -0.2, 0.2)), 1.5497207961345794e-09, 6.139278418970662e-09)
    output_weight = noise(seeds[7], (D, D), (max(D // 128, 8)) ** -0.5, 1.5, ((0, 32),), jnp.float32)
    output_mean = noise(seeds[8], (D, D), (0.011 / (D * FF) ** 0.5), 1.52587890625e-05, ((0, 32),), jnp.float32)
    output_square = jnp.clip(jnp.exp(math.log(1.2516974956522375e-10) - 1.3768155 * jax.random.uniform(seeds[9], (D, D), jnp.float32) ** block_scale(seeds[9], (D, D), ((0, 32),), -0.2, 0.2)), 3.1590462884478754e-11, 1.2516974956522375e-10)
    expand_weight = noise(seeds[10], (D, 2 * FF), D ** -0.5, 0.125, ((0, 32),), jnp.float32)
    expand_mean = noise(seeds[11], (D, 2 * FF), (0.037 / (D * FF) ** 0.5), 5.340576171875e-05, ((0, 32),), jnp.float32)
    expand_square = jnp.clip(jnp.exp(math.log(1.3709068324985196e-09) - 1.395028 * jax.random.uniform(seeds[12], (D, 2 * FF), jnp.float32) ** block_scale(seeds[12], (D, 2 * FF), ((0, 32),), -0.2, 0.2)), 3.3974648094847737e-10, 1.3709068324985196e-09)
    shrink_weight = noise(seeds[13], (D, FF), FF ** -0.5, 0.0625, ((0, 32),), jnp.float32)
    shrink_mean = noise(seeds[14], (D, FF), (0.072 / (D * FF) ** 0.5), 0.00010681152, ((0, 32),), jnp.float32)
    shrink_square = jnp.clip(jnp.exp(math.log(5.304813477380321e-09) - 1.397594 * jax.random.uniform(seeds[15], (D, FF), jnp.float32) ** block_scale(seeds[15], (D, FF), ((0, 32),), -0.2, 0.2)), 1.3113021779531664e-09, 5.304813477380321e-09)
    return {"tokens": tokens, "cotangent": cotangent, "positions": positions, "segments": segments, "joint_weight": joint_weight, "joint_mean": joint_mean, "joint_square": joint_square, "output_weight": output_weight, "output_mean": output_mean, "output_square": output_square, "expand_weight": expand_weight, "expand_mean": expand_mean, "expand_square": expand_square, "shrink_weight": shrink_weight, "shrink_mean": shrink_mean, "shrink_square": shrink_square}


@jax.custom_vjp
def low(v):
    return lax.optimization_barrier(v.astype(jnp.bfloat16)).astype(jnp.float32)

@jax.custom_vjp
def low_back(v):
    return v

def low_keep(v):
    return (low(v), None)

def low_pass(kept, grad):
    return (grad,)

def back_keep(v):
    return (v, None)

def back_low(kept, grad):
    return (low(grad),)
low.defvjp(low_keep, low_pass)
low_back.defvjp(back_keep, back_low)
highest = lax.Precision.HIGHEST
norm_epsilon = 1e-05
rope_base = 10000.0
clip_limit = 1.0
beta_first = 0.9
beta_second = 0.95
adam_epsilon = 1e-08
decay_rate = 0.1
main_rate = 0.02
output_rate = 0.2
masked_score = -1e+30

def layer_norm(values):
    centered = values - lax.optimization_barrier(jnp.mean(values, axis=-1, keepdims=True))
    return centered * lax.rsqrt(lax.optimization_barrier(jnp.mean(centered * centered, axis=-1, keepdims=True)) + norm_epsilon)

def rotation_tables(places, head_size):
    half_size = head_size // 2
    steps_index = jnp.arange(half_size).astype(jnp.float32)
    inverse = jnp.exp(steps_index * (-2.0 * math.log(rope_base) / head_size))
    angles = places.astype(jnp.float32)[:, None] * inverse[None, :]
    return (jnp.cos(angles)[:, None, :], jnp.sin(angles)[:, None, :])

def rotary(values, cosine, sine):
    half_size = values.shape[-1] // 2
    first_half = values[..., :half_size]
    second_half = values[..., half_size:]
    return jnp.concatenate([first_half * cosine - second_half * sine, second_half * cosine + first_half * sine], axis=-1)

def head_attention(query_head, key_head, value_head, allowed):
    score_scale = 1.0 / math.sqrt(query_head.shape[-1])
    scores = low_back(jnp.dot(query_head, key_head.T, precision=highest) * score_scale)
    masked = jnp.where(allowed, scores, masked_score)
    row_top = lax.optimization_barrier(jnp.max(masked, axis=-1, keepdims=True))
    exponent = jnp.exp(masked - row_top)
    probabilities = exponent / lax.optimization_barrier(jnp.sum(exponent, axis=-1, keepdims=True))
    return jnp.dot(low(probabilities), value_head, precision=highest)

def sequence_forward(token_values, joint_weight, output_weight, expand_weight, shrink_weight, places, documents):
    length = token_values.shape[0]
    model_width = token_values.shape[1]
    head_size = HEAD_DIM
    head_count = model_width // head_size
    hidden = shrink_weight.shape[1]
    first_norm = low(layer_norm(token_values))
    projected = jnp.dot(first_norm, low(joint_weight), precision=highest)
    query_raw = low_back(projected[:, :model_width])
    key_raw = low_back(projected[:, model_width:2 * model_width])
    value_raw = low_back(projected[:, 2 * model_width:])
    cosine, sine = rotation_tables(places, head_size)
    queries = low(rotary(query_raw.reshape(length, head_count, head_size), cosine, sine))
    key_rows = low(rotary(key_raw.reshape(length, head_count, head_size), cosine, sine))
    value_rows = low(value_raw.reshape(length, head_count, head_size))
    allowed = (documents[:, None] == documents[None, :]) & (places[None, :] <= places[:, None])
    attend = jax.checkpoint(lambda parts: head_attention(parts[0], parts[1], parts[2], allowed))
    mixed = lax.map(attend, (jnp.moveaxis(queries, 1, 0), jnp.moveaxis(key_rows, 1, 0), jnp.moveaxis(value_rows, 1, 0)))
    attended = low_back(low(jnp.moveaxis(mixed, 0, 1).reshape(length, model_width)))
    branch = low_back(jnp.dot(attended, low(output_weight).T, precision=highest))
    residual = token_values + branch
    second_norm = low(layer_norm(residual))
    expanded = jnp.dot(second_norm, low(expand_weight), precision=highest)
    up_part = low_back(expanded[:, :hidden])
    gate_part = low_back(expanded[:, hidden:])
    activated = low(gate_part * (1.0 / (1.0 + jnp.exp(-gate_part))) * up_part)
    return residual + jnp.dot(activated, low(shrink_weight).T, precision=highest)

def adam_update(weight, moment_one, moment_two, gradient, factor, step_rate):
    clipped = gradient * factor
    mean_new = beta_first * moment_one + (1.0 - beta_first) * clipped
    square_new = beta_second * moment_two + (1.0 - beta_second) * clipped * clipped
    mean_hat = mean_new / (1.0 - beta_first ** STEP)
    square_hat = square_new / (1.0 - beta_second ** STEP)
    weight_new = weight - step_rate * (mean_hat / (jnp.sqrt(square_hat) + adam_epsilon) + decay_rate * weight)
    return (weight_new, mean_new, square_new)

def reference(tokens, cotangent, positions, segments, joint_weight, joint_mean, joint_square, output_weight, output_mean, output_square, expand_weight, expand_mean, expand_square, shrink_weight, shrink_mean, shrink_square):
    masters = (joint_weight, output_weight, expand_weight, shrink_weight)

    def one_sequence(totals, scanned):
        token_rows, back_rows, place_row, document_row = scanned

        def layer_pass(token_values, joint_value, output_value, expand_value, shrink_value):
            return sequence_forward(token_values, joint_value, output_value, expand_value, shrink_value, place_row, document_row)
        result, pullback = jax.vjp(layer_pass, token_rows.astype(jnp.float32), *masters)
        gradients = pullback(back_rows.astype(jnp.float32))
        totals = tuple((total_sum + gradient for total_sum, gradient in zip(totals, gradients[1:])))
        return (totals, (result.astype(jnp.bfloat16), gradients[0]))
    empty_sums = tuple((jnp.zeros_like(weight) for weight in masters))
    grad_sums, (layer_output, input_grad) = lax.scan(one_sequence, empty_sums, (tokens, cotangent, positions, segments))
    squares = jnp.sum(grad_sums[0] * grad_sums[0]) + jnp.sum(grad_sums[1] * grad_sums[1]) + jnp.sum(grad_sums[2] * grad_sums[2]) + jnp.sum(grad_sums[3] * grad_sums[3])
    grad_norm = jnp.sqrt(squares)
    factor = jnp.minimum(1.0, clip_limit / (grad_norm + 1e-06))
    joint_new = adam_update(joint_weight, joint_mean, joint_square, grad_sums[0], factor, main_rate)
    output_new = adam_update(output_weight, output_mean, output_square, grad_sums[1], factor, output_rate)
    expand_new = adam_update(expand_weight, expand_mean, expand_square, grad_sums[2], factor, main_rate)
    shrink_new = adam_update(shrink_weight, shrink_mean, shrink_square, grad_sums[3], factor, main_rate)
    return (layer_output, input_grad, grad_norm, joint_new[0], joint_new[1], joint_new[2], output_new[0], output_new[1], output_new[2], expand_new[0], expand_new[1], expand_new[2], shrink_new[0], shrink_new[1], shrink_new[2])
```

```python
import math

import jax
import jax.numpy as jnp
from jax import lax
from jax.experimental import pallas as pl
from jax.experimental.pallas import tpu as pltpu
from jax.sharding import PartitionSpec as P

HEAD_DIM = 128
STEP = 10
LINE = 4
CORES = 2
QUERY_BLOCK = 256

norm_epsilon = 1e-05
rope_base = 10000.0
clip_limit = 1.0
beta_first = 0.9
beta_second = 0.95
adam_epsilon = 1e-08
decay_rate = 0.1
main_rate = 0.02
output_rate = 0.2
masked_score = -1e30

f32 = jnp.float32
bf16 = jnp.bfloat16


def layer_norm(values):
    centered = values - jnp.mean(values, axis=-1, keepdims=True)
    return centered * lax.rsqrt(
        jnp.mean(centered * centered, axis=-1, keepdims=True) + norm_epsilon
    )


def norm_backward(values, upstream):
    centered = values - jnp.mean(values, axis=-1, keepdims=True)
    inverse = lax.rsqrt(jnp.mean(centered * centered, axis=-1, keepdims=True) + norm_epsilon)
    normed = centered * inverse
    return inverse * (
        upstream
        - jnp.mean(upstream, axis=-1, keepdims=True)
        - normed * jnp.mean(upstream * normed, axis=-1, keepdims=True)
    )


def adam_update(weight, moment_one, moment_two, gradient, factor, step_rate):
    clipped = gradient * factor
    mean_new = beta_first * moment_one + (1.0 - beta_first) * clipped
    square_new = beta_second * moment_two + (1.0 - beta_second) * clipped * clipped
    mean_hat = mean_new / (1.0 - beta_first**STEP)
    square_hat = square_new / (1.0 - beta_second**STEP)
    weight_new = weight - step_rate * (
        mean_hat / (jnp.sqrt(square_hat) + adam_epsilon) + decay_rate * weight
    )
    return (weight_new, mean_new, square_new)


def ring_order(ranks):
    lines = ranks // LINE
    order = []
    for x in range(lines):
        places = range(LINE) if x % 2 == 0 else range(LINE - 1, -1, -1)
        order += [z * lines + x for z in places]
    return order


def ring_perms(ranks):
    order = ring_order(ranks)
    right = [(order[i], order[(i + 1) % ranks]) for i in range(ranks)]
    return right, [(b, a) for a, b in right]


def ring_gather(block, ranks):
    right, left = ring_perms(ranks)
    half = ranks // 2
    width = block.shape[1] // 2
    out = [None] * ranks
    out[0] = block
    up = down = block
    for step in range(1, half):
        up = lax.ppermute(up, "ctx", right)
        down = lax.ppermute(down, "ctx", left)
        out[-step % ranks] = up
        out[step] = down
    up = lax.ppermute(up[:, :width], "ctx", right)
    down = lax.ppermute(down[:, width:], "ctx", left)
    out[half] = jnp.concatenate([up, down], axis=1)
    return out


def ring_scatter(parts, ranks):
    right, left = ring_perms(ranks)
    half = ranks // 2
    width = parts[0].shape[1] // 2
    up = lax.ppermute(parts[half][:, :width], "ctx", right)
    down = lax.ppermute(parts[half][:, width:], "ctx", left)
    for step in range(half - 1, 0, -1):
        ahead = parts[step].astype(f32)
        behind = parts[-step].astype(f32)
        if step == half - 1:
            ahead = jnp.concatenate([ahead[:, :width] + up.astype(f32), ahead[:, width:]], 1)
            behind = jnp.concatenate([behind[:, :width], behind[:, width:] + down.astype(f32)], 1)
        else:
            ahead = ahead + up.astype(f32)
            behind = behind + down.astype(f32)
        up = lax.ppermute(ahead.astype(bf16), "ctx", right)
        down = lax.ppermute(behind.astype(bf16), "ctx", left)
    return parts[0].astype(f32) + up.astype(f32) + down.astype(f32)


def core_perm(shards):
    return [(i, i ^ 1) for i in range(shards)]


def y_perm(shards, step):
    rows = shards // CORES
    return [(i, ((i // CORES + step) % rows) * CORES + i % CORES) for i in range(shards)]


def shard_gather(block, shards):
    swap = core_perm(shards)
    out = []
    for step in range(shards // CORES):
        if step:
            block = lax.ppermute(block, "fsdp", y_perm(shards, -1))
        out += [block, lax.ppermute(block, "fsdp", swap)]
    return out


def shard_scatter(grad, shards):
    rows = grad.shape[0] // shards
    slabs = grad.reshape(shards // CORES, CORES, rows, grad.shape[1])
    other = lax.ppermute(slabs[:, 1], "fsdp", core_perm(shards))
    summed = (slabs[:, 0].astype(f32) + other.astype(f32)).astype(bf16)
    carried = summed[-1]
    for step in range(shards // CORES - 2, -1, -1):
        arrived = lax.ppermute(carried, "fsdp", y_perm(shards, 1))
        carried = (summed[step].astype(f32) + arrived.astype(f32)).astype(bf16)
    return carried


def visible(pos_col, seg_col, pos_row, seg_row):
    return (seg_col == seg_row) & (pos_row <= pos_col)


def soft_rows(query, key, allowed):
    score = lax.dot_general(query, key, (((1,), (1,)), ((), ())), preferred_element_type=f32)
    masked = jnp.where(allowed, score * (1.0 / math.sqrt(HEAD_DIM)), masked_score)
    top = jnp.max(masked, axis=-1, keepdims=True)
    exponent = jnp.exp(masked - top)
    return exponent * (1.0 / jnp.sum(exponent, axis=-1, keepdims=True))


def forward_kernel(pieces, *refs):
    x_ref = refs[0]
    w_refs = refs[1 : 1 + pieces]
    cos_ref, sin_ref, pos_col, seg_col, pos_row, seg_row = refs[1 + pieces : 7 + pieces]
    q_ref, k_ref, v_ref, o_ref = refs[7 + pieces :]
    length = x_ref.shape[0]
    depth = x_ref.shape[1] // pieces
    own = q_ref.shape[1]
    heads = own // HEAD_DIM
    block = QUERY_BLOCK

    @pl.loop(0, length // block)
    def _(i):
        rows = pl.ds(pl.multiple_of(i * block, block), block)
        total = jnp.zeros((block, 3 * own), f32)
        for piece in range(pieces):
            total = total + jnp.dot(
                x_ref[rows, piece * depth : (piece + 1) * depth],
                w_refs[piece][...],
                preferred_element_type=f32,
            )
        cosine, sine = cos_ref[rows, :], sin_ref[rows, :]
        for part, ref in ((0, q_ref), (1, k_ref)):
            for head in range(heads):
                start = part * own + head * HEAD_DIM
                raw = total[:, start : start + HEAD_DIM]
                turned = raw * cosine + pltpu.roll(raw, HEAD_DIM // 2, 1) * sine
                ref[rows, head * HEAD_DIM : (head + 1) * HEAD_DIM] = turned.astype(bf16)
        v_ref[rows, :] = total[:, 2 * own :].astype(bf16)

    @pl.loop(0, length // block)
    def _(i):
        rows = pl.ds(pl.multiple_of(i * block, block), block)
        allowed = visible(pos_col[rows, :], seg_col[rows, :], pos_row[...], seg_row[...])
        for head in range(heads):
            columns = slice(head * HEAD_DIM, (head + 1) * HEAD_DIM)
            probs = soft_rows(q_ref[rows, columns], k_ref[:, columns], allowed)
            mixed = jnp.dot(probs.astype(bf16), v_ref[:, columns], preferred_element_type=f32)
            o_ref[rows, columns] = mixed.astype(bf16)


def backward_kernel(
    q_ref, k_ref, v_ref, up_ref, cos_ref, sin_ref, pos_col, seg_col, pos_row, seg_row, out_ref, dk, dv
):
    length, own = q_ref.shape
    heads = own // HEAD_DIM
    block = QUERY_BLOCK
    scale = 1.0 / math.sqrt(HEAD_DIM)
    over_rows = (((0,), (0,)), ((), ()))
    dk[...] = jnp.zeros_like(dk)
    dv[...] = jnp.zeros_like(dv)

    def turn_back(grad, rows):
        return grad * cos_ref[rows, :] - pltpu.roll(grad, HEAD_DIM // 2, 1) * sin_ref[rows, :]

    @pl.loop(0, length // block)
    def _(i):
        rows = pl.ds(pl.multiple_of(i * block, block), block)
        allowed = visible(pos_col[rows, :], seg_col[rows, :], pos_row[...], seg_row[...])
        for head in range(heads):
            columns = slice(head * HEAD_DIM, (head + 1) * HEAD_DIM)
            query, upstream = q_ref[rows, columns], up_ref[rows, columns]
            key, value = k_ref[:, columns], v_ref[:, columns]
            probs = soft_rows(query, key, allowed)
            prob_grad = lax.dot_general(
                upstream, value, (((1,), (1,)), ((), ())), preferred_element_type=f32
            )
            inner = jnp.sum(probs * prob_grad, axis=-1, keepdims=True)
            score_grad = (probs * (prob_grad - inner)).astype(bf16)
            query_grad = jnp.dot(score_grad, key, preferred_element_type=f32) * scale
            out_ref[rows, columns] = turn_back(query_grad, rows).astype(bf16)
            dk[:, columns] += lax.dot_general(
                score_grad, query, over_rows, preferred_element_type=f32
            )
            dv[:, columns] += lax.dot_general(
                probs.astype(bf16), upstream, over_rows, preferred_element_type=f32
            )

    @pl.loop(0, length // block)
    def _(i):
        rows = pl.ds(pl.multiple_of(i * block, block), block)
        for head in range(heads):
            columns = slice(head * HEAD_DIM, (head + 1) * HEAD_DIM)
            place = slice(own + head * HEAD_DIM, own + (head + 1) * HEAD_DIM)
            out_ref[rows, place] = turn_back(dk[rows, columns] * scale, rows).astype(bf16)
        out_ref[rows, 2 * own :] = dv[rows, :].astype(bf16)


def attention_forward(x, weights, cosine, sine, places):
    length = x.shape[0]
    own = weights[0].shape[1] // 3
    heads = own // HEAD_DIM
    vmem = pl.BlockSpec(memory_space=pltpu.VMEM)
    piece = jax.ShapeDtypeStruct((length, own), bf16)
    flops = 2 * length * x.shape[1] * 3 * own + 4 * heads * length * length * HEAD_DIM
    return pl.pallas_call(
        lambda *refs: forward_kernel(len(weights), *refs),
        out_shape=[piece] * 4,
        in_specs=[vmem] * (7 + len(weights)),
        out_specs=[vmem] * 4,
        compiler_params=pltpu.CompilerParams(vmem_limit_bytes=48 * 2**20),
        cost_estimate=pl.CostEstimate(
            flops=flops,
            bytes_accessed=2 * (x.size + 3 * own * x.shape[1] + 4 * length * own),
            transcendentals=heads * length * length,
        ),
        name="attention_forward",
    )(x, *weights, cosine, sine, *places)


def attention_backward(queries, keys, values, upstream, cosine, sine, places):
    length, own = queries.shape
    heads = own // HEAD_DIM
    vmem = pl.BlockSpec(memory_space=pltpu.VMEM)
    return pl.pallas_call(
        backward_kernel,
        out_shape=jax.ShapeDtypeStruct((length, 3 * own), bf16),
        in_specs=[vmem] * 10,
        out_specs=vmem,
        scratch_shapes=[pltpu.VMEM((length, own), f32), pltpu.VMEM((length, own), f32)],
        compiler_params=pltpu.CompilerParams(vmem_limit_bytes=48 * 2**20),
        cost_estimate=pl.CostEstimate(
            flops=10 * heads * length * length * HEAD_DIM,
            bytes_accessed=2 * 7 * length * own,
            transcendentals=heads * length * length,
        ),
        name="attention_backward",
    )(queries, keys, values, upstream, cosine, sine, *places)


def body(ranks, shards):
    def run(
        tokens,
        cotangent,
        positions,
        segments,
        joint_weight,
        joint_mean,
        joint_square,
        output_weight,
        output_mean,
        output_square,
        expand_weight,
        expand_mean,
        expand_square,
        shrink_weight,
        shrink_mean,
        shrink_square,
    ):
        rank = lax.axis_index("ctx")
        shard = lax.axis_index("fsdp")
        count, width = tokens.shape[1], tokens.shape[2]
        hidden = shrink_weight.shape[1]
        own = width // ranks
        own_hidden = hidden // ranks
        rows = width // (ranks * shards)
        order = ring_order(ranks)
        place_of = [order.index(i) for i in range(ranks)]

        y_rows = shards // CORES
        own_y, own_core = shard // CORES, shard % CORES
        near = jnp.arange(shards)
        chunk_of = ((own_y + near // CORES) % y_rows) * CORES + (own_core ^ (near % CORES))
        chunk_back = ((jnp.arange(shards) // CORES - own_y) % y_rows) * CORES + (
            own_core ^ (jnp.arange(shards) % CORES)
        )

        def to_inner(values):
            split = values.reshape(count, ranks, shards, rows).transpose(2, 0, 1, 3)
            return jnp.take(split, chunk_of, axis=0).transpose(1, 0, 2, 3).reshape(count, width)

        def to_outer(values):
            split = values.reshape(count, shards, ranks, rows).transpose(1, 0, 2, 3)
            return jnp.take(split, chunk_back, axis=0).transpose(1, 2, 0, 3).reshape(count, width)

        def spread(weight, groups):
            split = weight.astype(bf16).reshape(rows, groups, ranks, -1).transpose(2, 0, 1, 3)
            split = split.reshape(ranks, rows, -1)
            moved = lax.all_to_all(split, "ctx", 0, 0, tiled=True)
            return shard_gather(moved.reshape(ranks * rows, -1), shards)

        def collect(grad, groups):
            summed = shard_scatter(grad, shards).reshape(ranks, rows, -1)
            moved = lax.all_to_all(summed, "ctx", 0, 0, tiled=True)
            moved = moved.reshape(ranks, rows, groups, -1).transpose(1, 2, 0, 3)
            return moved.reshape(rows, -1).astype(f32)

        joint_pieces = spread(joint_weight, 3)
        output_pieces = spread(output_weight, 1)
        expand_pieces = spread(expand_weight, 2)
        shrink_pieces = spread(shrink_weight, 1)
        joint_own = jnp.concatenate(joint_pieces, 0)
        output_own = jnp.concatenate(output_pieces, 0)
        expand_own = jnp.concatenate(expand_pieces, 0)
        shrink_own = jnp.concatenate(shrink_pieces, 0)

        ring = jnp.array(order, jnp.int32)
        here = jnp.array(place_of, jnp.int32)[rank]
        block_of = ring[(here + jnp.arange(ranks)) % ranks]
        pos = jnp.take(positions[0].reshape(ranks, count), block_of, axis=0).reshape(-1)
        seg = jnp.take(segments[0].reshape(ranks, count), block_of, axis=0).reshape(-1)
        places = (pos[:, None], seg[:, None], pos[None, :], seg[None, :])
        half = HEAD_DIM // 2
        inverse = jnp.exp(jnp.arange(half).astype(f32) * (-2.0 * math.log(rope_base) / HEAD_DIM))
        angles = pos.astype(f32)[:, None] * inverse[None, :]
        cosine, sine = jnp.cos(angles), jnp.sin(angles)
        cosine = jnp.concatenate([cosine, cosine], 1)
        sine = jnp.concatenate([-sine, sine], 1)

        def split_blocks(values):
            return [values[i * count : (i + 1) * count] for i in range(ranks)]

        token_rows = to_inner(tokens[0]).astype(f32)
        back_low = to_inner(cotangent[0])
        first_own = layer_norm(token_rows).astype(bf16)
        first_norm = jnp.concatenate(ring_gather(first_own, ranks), 0)
        queries, keys, values, attended = attention_forward(
            first_norm, joint_pieces, cosine, sine, places
        )
        branch = lax.dot_general(
            attended, output_own, (((1,), (1,)), ((), ())), preferred_element_type=f32
        ).astype(bf16)
        residual = token_rows + ring_scatter(split_blocks(branch), ranks)
        second_own = layer_norm(residual).astype(bf16)
        back_rows = jnp.concatenate(ring_gather(back_low, ranks), 0)
        second_norm = jnp.concatenate(ring_gather(second_own, ranks), 0)

        expanded = jnp.dot(second_norm, expand_own, preferred_element_type=f32)
        up_part, gate_part = expanded[:, :own_hidden], expanded[:, own_hidden:]
        sigma = 1.0 / (1.0 + jnp.exp(-gate_part))
        swish = gate_part * sigma
        activated = (swish * up_part).astype(bf16)
        act_grad = jnp.dot(back_rows, shrink_own, preferred_element_type=f32)
        up_grad = (act_grad * swish).astype(bf16)
        gate_grad = (act_grad * up_part * sigma * (1.0 + gate_part * (1.0 - sigma))).astype(bf16)
        upstream = jnp.concatenate([up_grad, gate_grad], axis=-1)
        second_part = lax.dot_general(
            upstream, expand_own, (((1,), (1,)), ((), ())), preferred_element_type=f32
        ).astype(bf16)
        second_grad = ring_scatter(split_blocks(second_part), ranks)
        shrunk = lax.dot_general(
            activated, shrink_own, (((1,), (1,)), ((), ())), preferred_element_type=f32
        ).astype(bf16)
        layer_inner = (residual + ring_scatter(split_blocks(shrunk), ranks)).astype(bf16)
        layer_output = to_outer(layer_inner)[None]

        over_tokens = (((0,), (0,)), ((), ()))

        def token_sum(left, right):
            return lax.dot_general(left, right, over_tokens, preferred_element_type=f32).astype(bf16)

        expand_grad = collect(token_sum(second_norm, upstream), 2)
        shrink_grad = collect(token_sum(back_rows, activated), 1)

        residual_grad = back_low.astype(f32) + norm_backward(residual, second_grad)
        branch_grad = jnp.concatenate(ring_gather(residual_grad.astype(bf16), ranks), 0)
        attended_grad = jnp.dot(branch_grad, output_own, preferred_element_type=f32).astype(bf16)
        joint_upstream = attention_backward(
            queries, keys, values, attended_grad, cosine, sine, places
        )
        first_part = lax.dot_general(
            joint_upstream, joint_own, (((1,), (1,)), ((), ())), preferred_element_type=f32
        ).astype(bf16)
        first_grad = ring_scatter(split_blocks(first_part), ranks)
        input_grad = to_outer(residual_grad + norm_backward(token_rows, first_grad))[None]
        output_grad = collect(token_sum(branch_grad, attended), 1)
        joint_grad = collect(token_sum(first_norm, joint_upstream), 3)

        squares = sum(
            jnp.sum(grad * grad) for grad in (joint_grad, output_grad, expand_grad, shrink_grad)
        )
        grad_norm = jnp.sqrt(lax.psum(squares, ("ctx", "fsdp")))
        factor = jnp.minimum(1.0, clip_limit / (grad_norm + 1e-06))
        joint_new = adam_update(
            joint_weight, joint_mean, joint_square, joint_grad, factor, main_rate
        )
        output_new = adam_update(
            output_weight, output_mean, output_square, output_grad, factor, output_rate
        )
        expand_new = adam_update(
            expand_weight, expand_mean, expand_square, expand_grad, factor, main_rate
        )
        shrink_new = adam_update(
            shrink_weight, shrink_mean, shrink_square, shrink_grad, factor, main_rate
        )
        return (
            layer_output,
            input_grad,
            grad_norm,
            *joint_new,
            *output_new,
            *expand_new,
            *shrink_new,
        )

    return run


def solution(mesh):
    tokens_spec = P("fsdp", "ctx", None)
    place_spec = P("fsdp", None)
    weight_spec = P(("ctx", "fsdp"), None)
    return jax.shard_map(
        body(mesh.shape["ctx"], mesh.shape["fsdp"]),
        mesh=mesh,
        in_specs=(tokens_spec, tokens_spec, place_spec, place_spec) + (weight_spec,) * 12,
        out_specs=(tokens_spec, tokens_spec, P()) + (weight_spec,) * 12,
        check_vma=False,
    )
```

```python
import math

import jax
import jax.numpy as jnp
from jax import lax
from jax.experimental import pallas as pl
from jax.experimental.pallas import tpu as pltpu
from jax.sharding import PartitionSpec as P

HEAD_DIM = 128
STEP = 10
LINE = 4
CORES = 2
QUERY_BLOCK = 256
ADAM_COLUMNS = 2048

norm_epsilon = 1e-05
rope_base = 10000.0
clip_limit = 1.0
beta_first = 0.9
beta_second = 0.95
adam_epsilon = 1e-08
decay_rate = 0.1
main_rate = 0.02
output_rate = 0.2
masked_score = -1e30

f32 = jnp.float32
bf16 = jnp.bfloat16


def layer_norm(values):
    centered = values - jnp.mean(values, axis=-1, keepdims=True)
    return centered * lax.rsqrt(
        jnp.mean(centered * centered, axis=-1, keepdims=True) + norm_epsilon
    )


def adam_update(weight, moment_one, moment_two, gradient, factor, step_rate):
    clipped = gradient * factor
    mean_new = beta_first * moment_one + (1.0 - beta_first) * clipped
    square_new = beta_second * moment_two + (1.0 - beta_second) * clipped * clipped
    mean_hat = mean_new / (1.0 - beta_first**STEP)
    square_hat = square_new / (1.0 - beta_second**STEP)
    weight_new = weight - step_rate * (
        mean_hat / (jnp.sqrt(square_hat) + adam_epsilon) + decay_rate * weight
    )
    return (weight_new, mean_new, square_new)


def ring_order(ranks):
    lines = ranks // LINE
    order = []
    for x in range(lines):
        places = range(LINE) if x % 2 == 0 else range(LINE - 1, -1, -1)
        order += [z * lines + x for z in places]
    return order


def ring_perms(ranks):
    order = ring_order(ranks)
    right = [(order[i], order[(i + 1) % ranks]) for i in range(ranks)]
    return right, [(b, a) for a, b in right]


brief = pl.CostEstimate(flops=10**6, bytes_accessed=10**5, transcendentals=0)


def anywhere(count):
    return [pl.BlockSpec(memory_space=pl.ANY)] * count


def in_vmem(count):
    return [pl.BlockSpec(memory_space=pltpu.VMEM)] * count


def like(values):
    return [jax.ShapeDtypeStruct(value.shape, value.dtype) for value in values]


def hold(*values):
    return pl.pallas_call(
        lambda *refs: None,
        out_shape=like(values),
        in_specs=anywhere(len(values)),
        out_specs=anywhere(len(values)),
        input_output_aliases={i: i for i in range(len(values))},
        name="hold",
    )(*values)


def pair_order(ranks):
    half = ranks // 2
    return [0] + [d for step in range(1, half) for d in (-step, step)] + [half]


def ring_gather(block, ranks, parts=1, arrived=None, beside=None):
    right, left = ring_perms(ranks)
    half = ranks // 2
    count, width = block.shape
    middle = width // 2
    size = width // parts
    up = [block[:, i * size : (i + 1) * size] for i in range(parts)]
    down = list(up)
    lists, mark = [], []
    for step in range(1, half):
        row = (2 * step - 1) * count
        lists.append([])
        for i in range(parts):
            up[i] = lax.ppermute(up[i], "ctx", right)
            down[i] = lax.ppermute(down[i], "ctx", left)
            lists[-1] += [(up[i], row, i * size), (down[i], row + count, i * size)]
        if parts == 1:
            also = beside(step) if beside else mark
            up[0], down[0], *_ = hold(up[0], down[0], *also)
            lists[-1] = [(up[0], row, 0), (down[0], row + count, 0)]
        if arrived:
            mark = arrived(step, lists[-1])
    first = up[0] if parts == 2 else up[0][:, :middle]
    last = down[1] if parts == 2 else down[0][:, middle:]
    first = lax.ppermute(first, "ctx", right)
    last = lax.ppermute(last, "ctx", left)
    row = (ranks - 1) * count
    ends = [(block, 0, 0), (first, row, 0), (last, row, middle)]
    if arrived:
        arrived(half, ends)
    return [ends] + lists


def flat(lists):
    return [block for blocks in lists for block in blocks]


def hold_ends(lists, *others):
    ends = lists[0][1:] + lists[-1]
    held = hold(*[array for array, *_ in ends], *others)
    ends = [(array, *place) for array, (_, *place) in zip(held, ends)]
    lists = [[lists[0][0]] + ends[:2]] + lists[1:-1] + [ends[2:]]
    return lists, held[len(ends) :]


def fetch_blocks(target, refs, places, sems):
    copies = []
    for index, (ref, (row, column)) in enumerate(zip(refs, places)):
        height, width = ref.shape
        place = target.at[row : row + height, column : column + width]
        copies.append(pltpu.make_async_copy(ref, place, sems.at[index]))
        copies[-1].start()
    return copies


def scatter_tick(up, down, up_part, down_part, waits):
    count = up.shape[0]
    parts = (up_part, down_part)
    sends = [jax.ShapeDtypeStruct((count, end - start), bf16) for _, _, start, end in parts]

    def kernel(*refs):
        up_out, down_out, token = refs[-3:]
        for ref, pair_ref, out, row, (_, column, start, end) in (
            (refs[0], refs[2], up_out, count, up_part),
            (refs[1], refs[3], down_out, 0, down_part),
        ):
            size = ref.shape[1]
            if size < end - start:
                out[...] = pair_ref[row : row + count, start:end]
            own = pair_ref[row : row + count, column : column + size]
            out[:, column - start : column - start + size] = (
                ref[...].astype(f32) + own.astype(f32)
            ).astype(bf16)
        token[...] = jnp.zeros_like(token)

    return pl.pallas_call(
        kernel,
        out_shape=sends + [jax.ShapeDtypeStruct((8, 128), f32)],
        in_specs=in_vmem(4) + anywhere(len(waits)),
        out_specs=in_vmem(3),
        name="scatter_tick",
    )(up, down, up_part[0], down_part[0], *waits)


class Scatter:
    def __init__(self, ranks, waits):
        self.right, self.left = ring_perms(ranks)
        self.waits, self.tokens = waits, []

    def send(self, up, down):
        return lax.ppermute(up, "ctx", self.right), lax.ppermute(down, "ctx", self.left)

    def add(self, state, up_part, down_part):
        turn = len(self.tokens)
        waiting = self.tokens[-1:] + list(self.waits(turn, self.tokens))
        up, down, token = scatter_tick(*state, up_part, down_part, waiting)
        self.tokens.append(token)
        return self.send(up, down)


def twin_scatter(low, high, ranks, waits=lambda turn, tokens: []):
    ring = Scatter(ranks, waits)
    half = ranks // 2
    count = low[0][0].shape[0]

    def part(side, step):
        blocks, start, end = side
        return (blocks[step], start, start, end)

    def columns(side, step):
        blocks, start, end = side
        return blocks[step][:, start:end]

    first = ring.send(columns(low, half), columns(high, half))
    second = ring.send(columns(high, half - 1)[count:], columns(low, half - 1)[:count])
    for step in range(half - 1, 0, -1):
        first = ring.add(first, part(low, step), part(high, step))
        if step > 1:
            second = ring.add(second, part(high, step - 1), part(low, step - 1))
    return (first[0], second[1]), (second[0], first[1])


def sum_everywhere(value, ranks, shards):
    held = jnp.full((8, 128), value, f32)
    for axis, size in (("fsdp", shards), ("ctx", ranks)):
        step = 1
        while step < size:
            held = held + lax.ppermute(held, axis, [(i, i ^ step) for i in range(size)])
            step *= 2
    return held[0, 0]


def core_perm(shards):
    return [(i, i ^ 1) for i in range(shards)]


def y_perm(shards, step):
    rows = shards // CORES
    return [(i, ((i // CORES + step) % rows) * CORES + i % CORES) for i in range(shards)]


def visible(pos_col, seg_col, pos_row, seg_row):
    return (seg_col == seg_row) & (pos_row <= pos_col)


def soft_rows(query, key, allowed):
    score = lax.dot_general(query, key, (((1,), (1,)), ((), ())), preferred_element_type=f32)
    masked = jnp.where(allowed, score * (1.0 / math.sqrt(HEAD_DIM)), masked_score)
    top = jnp.max(masked, axis=-1, keepdims=True)
    exponent = jnp.exp(masked - top)
    return exponent * (1.0 / jnp.sum(exponent, axis=-1, keepdims=True))


def project_kernel(places, pieces, *refs):
    blocks = refs[: len(places)]
    w_refs = refs[len(places) : len(places) + pieces]
    cos_ref, sin_ref, x_ref, q_ref, k_ref, v_ref, token, sems = refs[len(places) + pieces :]
    token[...] = jnp.zeros_like(token)
    length = x_ref.shape[0]
    depth = x_ref.shape[1] // pieces
    own = q_ref.shape[1]
    block = QUERY_BLOCK
    for copy in fetch_blocks(x_ref, blocks, places, sems):
        copy.wait()

    @pl.loop(0, length // block)
    def _(i):
        rows = pl.ds(pl.multiple_of(i * block, block), block)
        total = jnp.zeros((block, 3 * own), f32)
        for piece in range(pieces):
            total = total + jnp.dot(
                x_ref[rows, piece * depth : (piece + 1) * depth],
                w_refs[piece][:, : 3 * own],
                preferred_element_type=f32,
            )
        cosine, sine = cos_ref[rows, :], sin_ref[rows, :]
        for part, ref in ((0, q_ref), (1, k_ref)):
            for head in range(own // HEAD_DIM):
                start = part * own + head * HEAD_DIM
                raw = total[:, start : start + HEAD_DIM]
                turned = raw * cosine + pltpu.roll(raw, HEAD_DIM // 2, 1) * sine
                ref[rows, head * HEAD_DIM : (head + 1) * HEAD_DIM] = turned.astype(bf16)
        v_ref[rows, :] = total[:, 2 * own :].astype(bf16)


def head_kernel(head, q_ref, k_ref, v_ref, pos_col, seg_col, pos_row, seg_row, o_ref, token):
    token[...] = jnp.zeros_like(token)
    length = q_ref.shape[0]
    block = QUERY_BLOCK
    columns = slice(head * HEAD_DIM, (head + 1) * HEAD_DIM)

    @pl.loop(0, length // block)
    def _(i):
        rows = pl.ds(pl.multiple_of(i * block, block), block)
        allowed = visible(pos_col[rows, :], seg_col[rows, :], pos_row[...], seg_row[...])
        probs = soft_rows(q_ref[rows, columns], k_ref[:, columns], allowed)
        mixed = jnp.dot(probs.astype(bf16), v_ref[:, columns], preferred_element_type=f32)
        o_ref[rows, :] = mixed.astype(bf16)


def block_rows(ranks, count):
    ends = [0] + [(2 * step - 1) * count for step in range(1, ranks // 2 + 1)] + [ranks * count]
    return list(zip(ends[:-1], ends[1:]))


def product_blocks(source_ref, w_refs, columns, out_refs):
    start = 0
    for out_ref in out_refs:
        height, width = out_ref.shape
        depth = width // len(w_refs)
        for piece, w_ref in enumerate(w_refs):
            out_ref[:, piece * depth : (piece + 1) * depth] = lax.dot_general(
                source_ref[start : start + height, :],
                w_ref[:, columns],
                (((1,), (1,)), ((), ())),
                preferred_element_type=f32,
            ).astype(bf16)
        start += height


def branch_kernel(heads, pieces, *refs):
    o_refs = refs[:heads]
    w_refs = refs[heads : heads + pieces]
    attended_ref, *out_refs, token = refs[heads + pieces :]
    token[...] = jnp.zeros_like(token)
    own = heads * HEAD_DIM
    for head in range(heads):
        attended_ref[:, head * HEAD_DIM : (head + 1) * HEAD_DIM] = o_refs[head][...]
    product_blocks(attended_ref, w_refs, slice(3 * own, 4 * own), out_refs)


def backward_kernel(up_places, pieces, *refs):
    q_ref, k_ref, v_ref = refs[:3]
    up_blocks = refs[3 : 3 + len(up_places)]
    refs = refs[3 + len(up_places) :]
    w_refs = refs[:pieces]
    cos_ref, sin_ref, pos_col, seg_col, pos_row, seg_row = refs[pieces : 6 + pieces]
    up_ref, out_ref, *first_refs = refs[6 + pieces : -3]
    dk, dv, sems = refs[-3:]
    copies = fetch_blocks(up_ref, up_blocks, up_places, sems)
    length, own = q_ref.shape
    depth = up_ref.shape[1] // pieces
    heads = own // HEAD_DIM
    block = QUERY_BLOCK
    scale = 1.0 / math.sqrt(HEAD_DIM)
    over_rows = (((0,), (0,)), ((), ()))
    dk[...] = jnp.zeros_like(dk)
    dv[...] = jnp.zeros_like(dv)
    for copy in copies:
        copy.wait()

    def turn_back(grad, rows):
        return grad * cos_ref[rows, :] - pltpu.roll(grad, HEAD_DIM // 2, 1) * sin_ref[rows, :]

    @pl.loop(0, length // block)
    def _(i):
        rows = pl.ds(pl.multiple_of(i * block, block), block)
        allowed = visible(pos_col[rows, :], seg_col[rows, :], pos_row[...], seg_row[...])
        total = jnp.zeros((block, own), f32)
        for piece in range(pieces):
            total = total + jnp.dot(
                up_ref[rows, piece * depth : (piece + 1) * depth],
                w_refs[piece][:, 3 * own :],
                preferred_element_type=f32,
            )
        attended_grad = total.astype(bf16)
        for head in range(heads):
            columns = slice(head * HEAD_DIM, (head + 1) * HEAD_DIM)
            query, upstream = q_ref[rows, columns], attended_grad[:, columns]
            key, value = k_ref[:, columns], v_ref[:, columns]
            probs = soft_rows(query, key, allowed)
            prob_grad = lax.dot_general(
                upstream, value, (((1,), (1,)), ((), ())), preferred_element_type=f32
            )
            inner = jnp.sum(probs * prob_grad, axis=-1, keepdims=True)
            score_grad = (probs * (prob_grad - inner)).astype(bf16)
            query_grad = jnp.dot(score_grad, key, preferred_element_type=f32) * scale
            out_ref[rows, columns] = turn_back(query_grad, rows).astype(bf16)
            dk[:, columns] += lax.dot_general(
                score_grad, query, over_rows, preferred_element_type=f32
            )
            dv[:, columns] += lax.dot_general(
                probs.astype(bf16), upstream, over_rows, preferred_element_type=f32
            )

    @pl.loop(0, length // block)
    def _(i):
        rows = pl.ds(pl.multiple_of(i * block, block), block)
        for head in range(heads):
            columns = slice(head * HEAD_DIM, (head + 1) * HEAD_DIM)
            place = slice(own + head * HEAD_DIM, own + (head + 1) * HEAD_DIM)
            out_ref[rows, place] = turn_back(dk[rows, columns] * scale, rows).astype(bf16)
        out_ref[rows, 2 * own :] = dv[rows, :].astype(bf16)

    product_blocks(out_ref, w_refs, slice(0, 3 * own), first_refs)


def attention_forward(x_blocks, weights, cosine, sine, places, blocks):
    length, width = blocks[-1][1], x_blocks[0][0].shape[1]
    own = weights[0].shape[1] // 4
    heads = own // HEAD_DIM
    piece = jax.ShapeDtypeStruct((length, own), bf16)
    whole = jax.ShapeDtypeStruct((length, width), bf16)
    zeros = jax.ShapeDtypeStruct((8, 128), f32)
    params = pltpu.CompilerParams(vmem_limit_bytes=40 * 2**20)
    x, queries, keys, values, token = pl.pallas_call(
        lambda *refs: project_kernel([place for _, *place in x_blocks], len(weights), *refs),
        out_shape=[whole] + [piece] * 3 + [zeros],
        in_specs=anywhere(len(x_blocks)) + in_vmem(len(weights) + 2),
        out_specs=in_vmem(5),
        scratch_shapes=[pltpu.SemaphoreType.DMA((len(x_blocks),))],
        compiler_params=params,
        cost_estimate=brief,
        name="project",
    )(*[array for array, *_ in x_blocks], *weights, cosine, sine)
    yield [token]
    mixed = [
        pl.pallas_call(
            lambda *refs, head=head: head_kernel(head, *refs),
            out_shape=[jax.ShapeDtypeStruct((length, HEAD_DIM), bf16), zeros],
            in_specs=in_vmem(7),
            out_specs=in_vmem(2),
            compiler_params=params,
            cost_estimate=brief,
            name="attention_head",
        )(queries, keys, values, *places)
        for head in range(heads)
    ]
    yield [token for _, token in mixed]
    attended, *branch, token = pl.pallas_call(
        lambda *refs: branch_kernel(heads, len(weights), *refs),
        out_shape=[piece]
        + [jax.ShapeDtypeStruct((end - start, width), bf16) for start, end in blocks]
        + [zeros],
        in_specs=in_vmem(heads + len(weights)),
        out_specs=in_vmem(2 + len(blocks)),
        compiler_params=params,
        cost_estimate=brief,
        name="branch",
    )(*[head for head, _ in mixed], *weights)
    yield [token]
    yield x, queries, keys, values, attended, branch


def hidden_kernel(row, x_places, y_places, pieces, fresh, *refs):
    x_blocks, refs = refs[: len(x_places)], refs[len(x_places) :]
    y_blocks, refs = refs[: len(y_places)], refs[len(y_places) :]
    w_arrays, refs = refs[:pieces], refs[pieces if fresh else pieces + 4 :]
    *wholes, second_ref, shrunk_ref, mark_ref, x_ref, y_ref, active_ref, upstream_ref = refs[:-6]
    mark_ref[...] = jnp.zeros_like(mark_ref)
    w_ref, total_ref, sems, w_sems, x_sems, y_sems = refs[-6:]
    count, width = x_ref.shape
    hidden = active_ref.shape[1]
    depth = width // pieces
    block = min(hidden, 256)
    last = (((1,), (1,)), ((), ()))
    rows_in = fetch_blocks(x_ref, x_blocks, x_places, x_sems)
    rows_in += fetch_blocks(y_ref, y_blocks, y_places, y_sems)
    fetches = [
        pltpu.make_async_copy(array, w_ref.at[piece], w_sems.at[piece])
        for piece, array in enumerate(w_arrays)
    ]
    for fetch in fetches:
        fetch.start()
    for copy in rows_in:
        copy.wait()
    copies = [
        pltpu.make_async_copy(source, whole.at[row : row + count], sems.at[index])
        for index, (source, whole) in enumerate(
            zip((x_ref, y_ref, active_ref, upstream_ref), wholes)
        )
    ]
    copies[0].start()
    copies[1].start()
    for piece, fetch in enumerate(fetches):
        fetch.wait()
        rows = slice(piece * depth, (piece + 1) * depth)
        for source, columns in (
            (x_ref, slice(0, 2 * hidden)),
            (y_ref, slice(2 * hidden, 3 * hidden)),
        ):
            term = jnp.dot(
                source[:, rows], w_ref[piece, :, columns], preferred_element_type=f32
            )
            if piece:
                total_ref[:, columns] += term
            else:
                total_ref[:, columns] = term

    @pl.loop(0, hidden // block)
    def _(i):
        columns, gates, grads = (
            pl.ds(pl.multiple_of(part * hidden + i * block, block), block) for part in range(3)
        )
        up_part, gate_part, act_grad = total_ref[:, columns], total_ref[:, gates], total_ref[:, grads]
        sigma = 1.0 / (1.0 + jnp.exp(-gate_part))
        swish = gate_part * sigma
        active_ref[:, columns] = (swish * up_part).astype(bf16)
        upstream_ref[:, columns] = (act_grad * swish).astype(bf16)
        gate_grad = act_grad * up_part * sigma * (1.0 + gate_part * (1.0 - sigma))
        upstream_ref[:, gates] = gate_grad.astype(bf16)

    copies[2].start()
    copies[3].start()
    for piece in range(pieces):
        columns = slice(piece * depth, (piece + 1) * depth)
        second_ref[:, columns] = lax.dot_general(
            upstream_ref[...], w_ref[piece, :, : 2 * hidden], last, preferred_element_type=f32
        ).astype(bf16)
        shrunk_ref[:, columns] = lax.dot_general(
            active_ref[...], w_ref[piece, :, 2 * hidden :], last, preferred_element_type=f32
        ).astype(bf16)
    for copy in copies:
        copy.wait()


def hidden_pass(row, x_blocks, y_blocks, weights, length, wholes):
    width = weights[0].shape[0] * len(weights)
    count = sum(array.size for array, *_ in x_blocks) // width
    hidden = weights[0].shape[1] // 3
    kinds = [width, width, hidden, 2 * hidden]
    fresh = not wholes
    x_places, y_places = ([place for _, *place in blocks] for blocks in (x_blocks, y_blocks))
    given = len(x_blocks) + len(y_blocks) + len(weights)
    out = pl.pallas_call(
        lambda *refs: hidden_kernel(row, x_places, y_places, len(weights), fresh, *refs),
        out_shape=[jax.ShapeDtypeStruct((length, size), bf16) for size in kinds]
        + [jax.ShapeDtypeStruct((count, width), bf16)] * 2
        + [jax.ShapeDtypeStruct((8, 128), f32)],
        in_specs=anywhere(given + len(wholes)),
        out_specs=anywhere(4) + in_vmem(3),
        scratch_shapes=[pltpu.VMEM((count, size), bf16) for size in kinds]
        + [
            pltpu.VMEM((len(weights), *weights[0].shape), bf16),
            pltpu.VMEM((count, 3 * hidden), f32),
            pltpu.SemaphoreType.DMA((4,)),
            pltpu.SemaphoreType.DMA((len(weights),)),
            pltpu.SemaphoreType.DMA((len(x_blocks),)),
            pltpu.SemaphoreType.DMA((len(y_blocks),)),
        ],
        input_output_aliases={} if fresh else {given + i: i for i in range(4)},
        compiler_params=pltpu.CompilerParams(vmem_limit_bytes=40 * 2**20),
        cost_estimate=brief,
        name="hidden",
    )(*[array for array, *_ in x_blocks + y_blocks], *weights, *wholes)
    return out[:4], out[4], out[5], out[6]


def attention_backward(queries, keys, values, up_blocks, weights, cosine, sine, places, blocks):
    length, own = queries.shape
    width = up_blocks[0][0].shape[1]
    heads = own // HEAD_DIM
    return pl.pallas_call(
        lambda *refs: backward_kernel([place for _, *place in up_blocks], len(weights), *refs),
        out_shape=[
            jax.ShapeDtypeStruct((length, width), bf16),
            jax.ShapeDtypeStruct((length, 3 * own), bf16),
        ]
        + [jax.ShapeDtypeStruct((end - start, width), bf16) for start, end in blocks],
        in_specs=in_vmem(3) + anywhere(len(up_blocks)) + in_vmem(6 + len(weights)),
        out_specs=in_vmem(2 + len(blocks)),
        scratch_shapes=[
            pltpu.VMEM((length, own), f32),
            pltpu.VMEM((length, own), f32),
            pltpu.SemaphoreType.DMA((len(up_blocks),)),
        ],
        compiler_params=pltpu.CompilerParams(vmem_limit_bytes=48 * 2**20),
        cost_estimate=brief,
        name="attention_backward",
    )(
        queries,
        keys,
        values,
        *[array for array, *_ in up_blocks],
        *weights,
        cosine,
        sine,
        *places,
    )


def normed_rows(values):
    centered = values - jnp.mean(values, axis=-1, keepdims=True)
    inverse = lax.rsqrt(jnp.mean(centered * centered, axis=-1, keepdims=True) + norm_epsilon)
    return centered * inverse, inverse


def norm_back_rows(values, upstream):
    normed, inverse = normed_rows(values)
    return inverse * (
        upstream
        - jnp.mean(upstream, axis=-1, keepdims=True)
        - normed * jnp.mean(upstream * normed, axis=-1, keepdims=True)
    )


def row_call(kernel, name, kinds, *arrays):
    shape = arrays[0].shape

    def run(*refs):
        refs[-1][...] = jnp.zeros_like(refs[-1])
        kernel(*refs[:-1])

    return pl.pallas_call(
        run,
        out_shape=[jax.ShapeDtypeStruct(shape, kind) for kind in kinds]
        + [jax.ShapeDtypeStruct((8, 128), f32)],
        in_specs=in_vmem(len(arrays)),
        out_specs=in_vmem(len(kinds) + 1),
        name=name,
    )(*arrays)


def wide(*refs):
    total = refs[0][...].astype(f32)
    for ref in refs[1:]:
        total = total + ref[...].astype(f32)
    return total


def join_kernel(token_ref, own_ref, up0, down0, up1, down1, residual_ref, norm_ref):
    middle = own_ref.shape[1] // 2
    for columns, refs in ((slice(0, middle), (up0, down0)), (slice(middle, None), (up1, down1))):
        residual_ref[:, columns] = token_ref[:, columns].astype(f32) + (
            own_ref[:, columns].astype(f32) + wide(*refs)
        )
    norm_ref[...] = normed_rows(residual_ref[...])[0].astype(bf16)


def turn_kernel(residual_ref, back_ref, own_ref, up0, down0, up1, down1, grad_ref, low_ref):
    upstream = own_ref[...].astype(f32) + jnp.concatenate([wide(up0, down0), wide(up1, down1)], 1)
    grad = back_ref[...].astype(f32) + norm_back_rows(residual_ref[...], upstream)
    grad_ref[...] = grad
    low_ref[...] = grad.astype(bf16)


def last_kernel(token_ref, grad_ref, residual_ref, own0, up0, down0, own1, up1, down1, in_ref, out_ref):
    in_ref[...] = grad_ref[...] + norm_back_rows(token_ref[...].astype(f32), wide(own0, up0, down0))
    out_ref[...] = (residual_ref[...] + wide(own1, up1, down1)).astype(bf16)


def weight_term(shards, k, products, adds=(), waits=()):
    length, width = products[0][0].shape
    depth = width // shards
    block = min(right.shape[1] for _, right in products)
    steps = [right.shape[1] // block for _, right in products]
    firsts = [sum(steps[:i]) for i in range(len(steps))]

    def kernel(*refs):
        out, token = refs[-2:]
        more = refs[2 * len(products) : 2 * len(products) + len(adds)]
        step = pl.program_id(0)
        token[...] = jnp.zeros_like(token)
        for index, first in enumerate(firsts):

            @pl.when((step >= first) & (step < first + steps[index]))
            def _():
                total = lax.dot_general(
                    refs[2 * index][...],
                    refs[2 * index + 1][...],
                    (((0,), (0,)), ((), ())),
                    preferred_element_type=f32,
                )
                out[...] = total.astype(bf16)
                for ref, (row, height) in zip(more, places):
                    rows = slice(row, row + height)
                    out[rows, :] = (total[rows, :] + ref[...].astype(f32)).astype(bf16)

    specs, arrays = [], []
    for (left, right), first, size in zip(products, firsts, steps):
        specs.append(pl.BlockSpec((length, depth), lambda n: (0, k)))
        specs.append(
            pl.BlockSpec(
                (length, block),
                lambda n, first=first, size=size: (0, jnp.clip(n - first, 0, size - 1)),
            )
        )
        arrays += [left, right]
    places = [(row, array.shape[0]) for array, row in adds]
    flat_block = pl.BlockSpec((depth, block), lambda n: (0, n))
    return pl.pallas_call(
        kernel,
        grid=(sum(steps),),
        out_shape=[
            jax.ShapeDtypeStruct((depth, sum(steps) * block), bf16),
            jax.ShapeDtypeStruct((8, 128), f32),
        ],
        in_specs=specs
        + [pl.BlockSpec((height, block), lambda n: (0, n)) for _, height in places]
        + anywhere(len(waits)),
        out_specs=[flat_block, pl.BlockSpec((8, 128), lambda n: (0, 0))],
        compiler_params=pltpu.CompilerParams(vmem_limit_bytes=48 * 2**20),
        cost_estimate=brief,
        name="weight_term",
    )(*arrays, *[array for array, _ in adds], *waits)


def adam_kernel(rate, factor_ref, w_ref, m_ref, v_ref, g_ref, w_out, m_out, v_out):
    ranks, _, block = g_ref.shape
    for rank in range(ranks):
        columns = slice(rank * block, (rank + 1) * block)
        w_out[:, columns], m_out[:, columns], v_out[:, columns] = adam_update(
            w_ref[:, columns],
            m_ref[:, columns],
            v_ref[:, columns],
            g_ref[rank].astype(f32),
            factor_ref[0, 0],
            rate,
        )


def adam_step(weight, mean, square, grad, first, groups, factor, rate):
    ranks, rows, _ = grad.shape
    block = weight.shape[1] // (groups * ranks)
    held = max(1, min(ranks, ADAM_COLUMNS // block))
    steps = ranks // held
    flat = pl.BlockSpec((rows, held * block), lambda g, r: (0, g * steps + r))
    shape = jax.ShapeDtypeStruct(weight.shape, f32)
    return pl.pallas_call(
        lambda *refs: adam_kernel(rate, *refs),
        grid=(groups, steps),
        out_shape=[shape] * 3,
        in_specs=[
            pl.BlockSpec(memory_space=pltpu.SMEM),
            flat,
            flat,
            flat,
            pl.BlockSpec((held, rows, block), lambda g, r: (r, 0, first + g)),
        ],
        out_specs=[flat] * 3,
        compiler_params=pltpu.CompilerParams(vmem_limit_bytes=56 * 2**20),
        cost_estimate=brief,
        name="adam_step",
    )(factor.reshape(1, 1), weight, mean, square, grad)


def body(ranks, shards):
    def run(
        tokens,
        cotangent,
        positions,
        segments,
        joint_weight,
        joint_mean,
        joint_square,
        output_weight,
        output_mean,
        output_square,
        expand_weight,
        expand_mean,
        expand_square,
        shrink_weight,
        shrink_mean,
        shrink_square,
    ):
        shard = lax.axis_index("fsdp")
        count, width = tokens.shape[1], tokens.shape[2]
        hidden = shrink_weight.shape[1]
        own = width // ranks
        own_hidden = hidden // ranks
        rows = width // (ranks * shards)
        y_rows = shards // CORES
        near_table = [
            [((f // CORES + k // CORES) % y_rows) * CORES + (f % CORES ^ k % CORES) for k in range(shards)]
            for f in range(shards)
        ]
        back_table = [[row.index(f) for f in range(shards)] for row in near_table]
        chunk_of = lax.dynamic_index_in_dim(jnp.array(near_table, jnp.int32), shard, 0, False)
        chunk_back = lax.dynamic_index_in_dim(jnp.array(back_table, jnp.int32), shard, 0, False)

        def to_inner(values):
            split = values.reshape(count, ranks, shards, rows).transpose(2, 0, 1, 3)
            return jnp.take(split, chunk_of, axis=0).transpose(1, 0, 2, 3).reshape(count, width)

        def to_outer(values):
            split = values.reshape(count, shards, ranks, rows).transpose(1, 0, 2, 3)
            return jnp.take(split, chunk_back, axis=0).transpose(1, 2, 0, 3).reshape(count, width)

        def columns_of(weight, groups):
            split = weight.astype(bf16).reshape(rows, groups, ranks, -1).transpose(2, 0, 1, 3)
            return split.reshape(ranks * rows, -1)

        def exchange(split):
            moved = lax.all_to_all(split.reshape(ranks, rows, -1), "ctx", 0, 0, tiled=True)
            return moved.reshape(ranks * rows, -1)

        def by_rank(moved):
            return moved.reshape(ranks, rows, -1)

        ahead, back = y_perm(shards, 1), y_perm(shards, -1)
        swap = core_perm(shards)

        def swapped(value):
            return lax.ppermute(value, "fsdp", swap)

        def across_y(block):
            blocks = [block]
            for _ in range(y_rows - 1):
                blocks.append(lax.ppermute(blocks[-1], "fsdp", back))
            return blocks

        def with_cores(blocks):
            return [piece for block in blocks for piece in (block, swapped(block))]

        token_low = to_inner(tokens[0])
        back_low = to_inner(cotangent[0])
        joint_split = columns_of(joint_weight, 3)
        output_split = columns_of(output_weight, 1)
        near_moved = exchange(jnp.concatenate([joint_split, output_split], 1))
        far_split = jnp.concatenate([columns_of(expand_weight, 2), columns_of(shrink_weight, 1)], 1)
        near_moved, far_split = hold(near_moved, far_split)
        far_moved = exchange(far_split)
        near_blocks = across_y(near_moved)

        order = ring_order(ranks)
        block_table = [
            [order[(order.index(i) + d) % ranks] for d in pair_order(ranks)] for i in range(ranks)
        ]
        block_of = lax.dynamic_index_in_dim(
            jnp.array(block_table, jnp.int32), lax.axis_index("ctx"), 0, False
        )
        pos = jnp.take(positions[0].reshape(ranks, count), block_of, axis=0).reshape(-1)
        seg = jnp.take(segments[0].reshape(ranks, count), block_of, axis=0).reshape(-1)
        places = (pos[:, None], seg[:, None], pos[None, :], seg[None, :])
        turn = HEAD_DIM // 2
        inverse = jnp.exp(jnp.arange(turn).astype(f32) * (-2.0 * math.log(rope_base) / HEAD_DIM))
        angles = pos.astype(f32)[:, None] * inverse[None, :]
        cosine, sine = jnp.cos(angles), jnp.sin(angles)
        cosine = jnp.concatenate([cosine, cosine], 1)
        sine = jnp.concatenate([-sine, sine], 1)

        def collect(products):
            total = None
            waits = yield
            for step in range(y_rows - 1, -1, -1):
                term, token = weight_term(shards, step * CORES + 1, products, (), waits)
                height = term.shape[0] // 4
                adds = [(swapped(term[row : row + height]), row) for row in range(0, 4 * height, height)]
                waits = yield token
                term, token = weight_term(shards, step * CORES, products, adds, waits)
                if total is not None:
                    term = (term.astype(f32) + total.astype(f32)).astype(bf16)
                if step:
                    total = lax.ppermute(term, "fsdp", ahead)
                    waits = yield token
            yield term

        def finish(work):
            result = None
            while True:
                try:
                    result = work.send([])
                except StopIteration:
                    return result

        def collect_all(products):
            work = collect(products)
            next(work)
            return finish(work)

        def square_sum(grad):
            return jnp.sum(jnp.square(grad.astype(f32)))

        first_own = layer_norm(token_low.astype(f32)).astype(bf16)
        first_own, far_moved, back_low, *near_blocks[1:] = hold(
            first_own, far_moved, back_low, *near_blocks[1:]
        )
        near = with_cores(near_blocks)
        far_blocks = across_y(far_moved)
        first_blocks = ring_gather(first_own, ranks, 2)
        near_core = swapped(far_moved)
        first_blocks, (back_low, near_core) = hold_ends(first_blocks, back_low, near_core)
        blocks = block_rows(ranks, count)
        work = attention_forward(flat(first_blocks), near, cosine, sine, places, blocks)
        back_blocks = ring_gather(
            back_low, ranks, beside=lambda step: next(work) if step <= 3 else []
        )
        first_norm, queries, keys, values, attended, branch = list(work)[-1]
        back_blocks, held = hold_ends(back_blocks, branch[-1], *far_blocks[1:])
        branch[-1], *far_blocks[1:] = held
        cores = [near_core] + [swapped(block) for block in far_blocks[1:]]
        far = [piece for pair in zip(far_blocks, cores) for piece in pair]
        middle = width // 2
        sums = twin_scatter(
            (branch, 0, middle),
            (branch, middle, width),
            ranks,
            lambda turn, _: cores[1:] if turn == 2 else [],
        )
        residual, second_own, _ = row_call(
            join_kernel, "join", (f32, bf16), token_low, branch[0], *sums[0], *sums[1]
        )

        half = ranks // 2
        length = ranks * count
        wholes, terms, shrunk = [], [None] * (half + 1), [None] * (half + 1)

        def arrived(step, x_blocks):
            first = x_blocks[0][1] if step < half else 0
            far_row = (ranks - 1) * count

            def local(given):
                return [
                    (array, count if row == far_row and step == half else row - first, column)
                    for array, row, column in given
                ]

            y_blocks = back_blocks[step % half]
            start = 2 * (step - 1) * count
            wholes[:], second, out, mark = hidden_pass(
                start, local(x_blocks), local(y_blocks), far, length, list(wholes)
            )
            if step < half:
                terms[step], shrunk[step] = second, out
            else:
                terms[0], terms[half] = second[:count], second[count:]
                shrunk[0], shrunk[half] = out[:count], out[count:]
            return [mark]

        ring_gather(second_own, ranks, 1, arrived)
        second_norm, back_rows, activated, upstream = wholes
        far_work = collect([(second_norm, upstream), (back_rows, activated)])
        next(far_work)

        def first_half(turn, tokens):
            return [far_work.send([tokens[turn - 2]])] if turn in (2, 4) and y_rows > 1 else []

        sums = twin_scatter((terms, 0, middle), (terms, middle, width), ranks, first_half)
        residual_grad, branch_low, mark = row_call(
            turn_kernel, "turn", (f32, bf16), residual, back_low, terms[0], *sums[0], *sums[1]
        )

        def second_half(step):
            return [far_work.send([mark])] if step == 1 else []

        branch_blocks = ring_gather(branch_low, ranks, beside=second_half)
        far_grad = finish(far_work)
        branch_blocks, (far_grad,) = hold_ends(branch_blocks, far_grad)
        far_back = exchange(far_grad)
        branch_grad, joint_upstream, *first_part = attention_backward(
            queries, keys, values, flat(branch_blocks), near, cosine, sine, places, blocks
        )
        near_grad = collect_all([(first_norm, joint_upstream), (branch_grad, attended)])
        near_grad, far_back = hold(near_grad, far_back)
        near_back = exchange(near_grad)
        squares = square_sum(near_back) + square_sum(far_back)
        total = sum_everywhere(squares, ranks, shards)
        first_part[-1], near_back = hold(first_part[-1], near_back)
        grad_norm = jnp.sqrt(total)
        factor = jnp.minimum(1.0, clip_limit / (grad_norm + 1e-06))
        joint_new = adam_step(
            joint_weight, joint_mean, joint_square, by_rank(near_back), 0, 3, factor, main_rate
        )
        output_new = adam_step(
            output_weight, output_mean, output_square, by_rank(near_back), 3, 1, factor, output_rate
        )
        expand_new = adam_step(
            expand_weight, expand_mean, expand_square, by_rank(far_back), 0, 2, factor, main_rate
        )
        shrink_new = adam_step(
            shrink_weight, shrink_mean, shrink_square, by_rank(far_back), 2, 1, factor, main_rate
        )
        sums = twin_scatter(
            (first_part, 0, width),
            (shrunk, 0, width),
            ranks,
            lambda turn, _: {2: joint_new + output_new, 3: shrink_new, 4: expand_new}.get(turn, []),
        )
        input_inner, layer_inner, _ = row_call(
            last_kernel,
            "last",
            (f32, bf16),
            token_low,
            residual_grad,
            residual,
            first_part[0],
            *sums[0],
            shrunk[0],
            *sums[1],
        )
        input_grad = to_outer(input_inner)[None]
        layer_output = to_outer(layer_inner)[None]
        return (
            layer_output,
            input_grad,
            grad_norm,
            *joint_new,
            *output_new,
            *expand_new,
            *shrink_new,
        )

    return run


def solution(mesh):
    tokens_spec = P("fsdp", "ctx", None)
    place_spec = P("fsdp", None)
    weight_spec = P(("ctx", "fsdp"), None)
    return jax.shard_map(
        body(mesh.shape["ctx"], mesh.shape["fsdp"]),
        mesh=mesh,
        in_specs=(tokens_spec, tokens_spec, place_spec, place_spec) + (weight_spec,) * 12,
        out_specs=(tokens_spec, tokens_spec, P()) + (weight_spec,) * 12,
        check_vma=False,
    )
```

```python
import math

import jax
import jax.numpy as jnp
from jax import lax
from jax.experimental import pallas as pl
from jax.experimental.pallas import tpu as pltpu
from jax.sharding import PartitionSpec as P

HEAD_DIM = 128
STEP = 10
LINE = 4
CORES = 2
QUERY_BLOCK = 256
ADAM_COLUMNS = 2048
KERNEL_VMEM = 60 * 2**20

norm_epsilon = 1e-05
rope_base = 10000.0
clip_limit = 1.0
beta_first = 0.9
beta_second = 0.95
adam_epsilon = 1e-08
decay_rate = 0.1
main_rate = 0.02
output_rate = 0.2
masked_score = -1e30

f32 = jnp.float32
bf16 = jnp.bfloat16


def layer_norm(values):
    centered = values - jnp.mean(values, axis=-1, keepdims=True)
    return centered * lax.rsqrt(
        jnp.mean(centered * centered, axis=-1, keepdims=True) + norm_epsilon
    )


def adam_update(weight, moment_one, moment_two, gradient, factor, step_rate):
    clipped = gradient * factor
    mean_new = beta_first * moment_one + (1.0 - beta_first) * clipped
    square_new = beta_second * moment_two + (1.0 - beta_second) * clipped * clipped
    mean_hat = mean_new / (1.0 - beta_first**STEP)
    square_hat = square_new / (1.0 - beta_second**STEP)
    weight_new = weight - step_rate * (
        mean_hat / (jnp.sqrt(square_hat) + adam_epsilon) + decay_rate * weight
    )
    return (weight_new, mean_new, square_new)


def ring_order(ranks):
    lines = ranks // LINE
    order = []
    for x in range(lines):
        places = range(LINE) if x % 2 == 0 else range(LINE - 1, -1, -1)
        order += [z * lines + x for z in places]
    return order


def ring_perms(ranks):
    order = ring_order(ranks)
    right = [(order[i], order[(i + 1) % ranks]) for i in range(ranks)]
    return right, [(b, a) for a, b in right]


brief = pl.CostEstimate(flops=10**6, bytes_accessed=10**5, transcendentals=0)


def anywhere(count):
    return [pl.BlockSpec(memory_space=pl.ANY)] * count


def in_vmem(count):
    return [pl.BlockSpec(memory_space=pltpu.VMEM)] * count


def like(values):
    return [jax.ShapeDtypeStruct(value.shape, value.dtype) for value in values]


def hold(*values):
    return pl.pallas_call(
        lambda *refs: None,
        out_shape=like(values),
        in_specs=anywhere(len(values)),
        out_specs=anywhere(len(values)),
        input_output_aliases={i: i for i in range(len(values))},
        name="hold",
    )(*values)


def pair_order(ranks):
    half = ranks // 2
    return [0] + [d for step in range(1, half) for d in (-step, step)] + [half]


def ring_gather(block, ranks, parts=1, arrived=None, beside=None, mark=()):
    right, left = ring_perms(ranks)
    half = ranks // 2
    count, width = block.shape
    middle = width // 2
    size = width // parts
    up = [block[:, i * size : (i + 1) * size] for i in range(parts)]
    down = list(up)
    lists = []
    for step in range(1, half):
        row = (2 * step - 1) * count
        lists.append([])
        for i in range(parts):
            up[i] = lax.ppermute(up[i], "ctx", right)
            down[i] = lax.ppermute(down[i], "ctx", left)
            lists[-1] += [(up[i], row, i * size), (down[i], row + count, i * size)]
        if parts == 1:
            also = beside(step) if beside else mark
            up[0], down[0], *_ = hold(up[0], down[0], *also)
            lists[-1] = [(up[0], row, 0), (down[0], row + count, 0)]
        if arrived:
            mark = arrived(step, lists[-1])
    first = up[0] if parts == 2 else up[0][:, :middle]
    last = down[1] if parts == 2 else down[0][:, middle:]
    first = lax.ppermute(first, "ctx", right)
    last = lax.ppermute(last, "ctx", left)
    row = (ranks - 1) * count
    ends = [(block, 0, 0), (first, row, 0), (last, row, middle)]
    if arrived:
        arrived(half, ends)
    return [ends] + lists


def flat(lists):
    return [block for blocks in lists for block in blocks]


def hold_ends(lists, *others):
    ends = lists[0][1:] + lists[-1]
    held = hold(*[array for array, *_ in ends], *others)
    ends = [(array, *place) for array, (_, *place) in zip(held, ends)]
    lists = [[lists[0][0]] + ends[:2]] + lists[1:-1] + [ends[2:]]
    return lists, held[len(ends) :]


def fetch_blocks(target, refs, places, sems):
    copies = []
    for index, (ref, (row, column)) in enumerate(zip(refs, places)):
        height, width = ref.shape
        place = target.at[row : row + height, column : column + width]
        copies.append(pltpu.make_async_copy(ref, place, sems.at[index]))
        copies[-1].start()
    return copies


def scatter_tick(up, down, up_part, down_part, waits):
    count = up.shape[0]
    parts = (up_part, down_part)
    sends = [jax.ShapeDtypeStruct((count, end - start), bf16) for _, _, start, end in parts]

    def kernel(*refs):
        up_out, down_out, token = refs[-3:]
        for ref, pair_ref, out, row, (_, column, start, end) in (
            (refs[0], refs[2], up_out, count, up_part),
            (refs[1], refs[3], down_out, 0, down_part),
        ):
            size = ref.shape[1]
            if size < end - start:
                out[...] = pair_ref[row : row + count, start:end]
            own = pair_ref[row : row + count, column : column + size]
            out[:, column - start : column - start + size] = (
                ref[...].astype(f32) + own.astype(f32)
            ).astype(bf16)
        token[...] = jnp.zeros_like(token)

    return pl.pallas_call(
        kernel,
        out_shape=sends + [jax.ShapeDtypeStruct((8, 128), f32)],
        in_specs=in_vmem(4) + anywhere(len(waits)),
        out_specs=in_vmem(3),
        compiler_params=pltpu.CompilerParams(vmem_limit_bytes=KERNEL_VMEM),
        name="scatter_tick",
    )(up, down, up_part[0], down_part[0], *waits)


class Scatter:
    def __init__(self, ranks, waits):
        self.right, self.left = ring_perms(ranks)
        self.waits, self.tokens = waits, []

    def send(self, up, down):
        return lax.ppermute(up, "ctx", self.right), lax.ppermute(down, "ctx", self.left)

    def add(self, state, up_part, down_part):
        turn = len(self.tokens)
        waiting = self.tokens[-1:] + list(self.waits(turn, self.tokens))
        up, down, token = scatter_tick(*state, up_part, down_part, waiting)
        self.tokens.append(token)
        return self.send(up, down)


def first_sends(low, high):
    half = len(low[0]) - 1
    count = low[0][0].shape[0]

    def columns(side, step):
        blocks, start, end = side
        return blocks[step][:, start:end]

    return [
        columns(low, half),
        columns(high, half),
        columns(high, half - 1)[count:],
        columns(low, half - 1)[:count],
    ]


def twin_scatter(low, high, sends, ranks, waits=lambda turn, tokens: []):
    ring = Scatter(ranks, waits)

    def part(side, step):
        blocks, start, end = side
        return (blocks[step], start, start, end)

    first = ring.send(sends[0], sends[1])
    second = ring.send(sends[2], sends[3])
    for step in range(ranks // 2 - 1, 0, -1):
        first = ring.add(first, part(low, step), part(high, step))
        if step > 1:
            second = ring.add(second, part(high, step - 1), part(low, step - 1))
    return (first[0], second[1]), (second[0], first[1])


def sum_everywhere(value, ranks, shards):
    held = jnp.full((8, 128), value, f32)
    for axis, size in (("fsdp", shards), ("ctx", ranks)):
        step = 1
        while step < size:
            held = held + lax.ppermute(held, axis, [(i, i ^ step) for i in range(size)])
            step *= 2
    return held


def core_perm(shards):
    return [(i, i ^ 1) for i in range(shards)]


def y_perm(shards, step):
    rows = shards // CORES
    return [(i, ((i // CORES + step) % rows) * CORES + i % CORES) for i in range(shards)]


def visible(pos_col, seg_col, pos_row, seg_row):
    return (seg_col == seg_row) & (pos_row <= pos_col)


def soft_rows(query, key, allowed):
    score = lax.dot_general(query, key, (((1,), (1,)), ((), ())), preferred_element_type=f32)
    masked = jnp.where(allowed, score * (1.0 / math.sqrt(HEAD_DIM)), masked_score)
    top = jnp.max(masked, axis=-1, keepdims=True)
    exponent = jnp.exp(masked - top)
    return exponent * (1.0 / jnp.sum(exponent, axis=-1, keepdims=True))


def project_kernel(places, pieces, *refs):
    blocks = refs[: len(places)]
    w_refs = refs[len(places) : len(places) + pieces]
    cos_ref, sin_ref, x_ref, q_ref, k_ref, v_ref, token, sems = refs[len(places) + pieces :]
    token[...] = jnp.zeros_like(token)
    length = x_ref.shape[0]
    depth = x_ref.shape[1] // pieces
    own = q_ref.shape[1]
    block = QUERY_BLOCK
    for copy in fetch_blocks(x_ref, blocks, places, sems):
        copy.wait()

    @pl.loop(0, length // block)
    def _(i):
        rows = pl.ds(pl.multiple_of(i * block, block), block)
        total = jnp.zeros((block, 3 * own), f32)
        for piece in range(pieces):
            total = total + jnp.dot(
                x_ref[rows, piece * depth : (piece + 1) * depth],
                w_refs[piece][:, : 3 * own],
                preferred_element_type=f32,
            )
        cosine, sine = cos_ref[rows, :], sin_ref[rows, :]
        for part, ref in ((0, q_ref), (1, k_ref)):
            for head in range(own // HEAD_DIM):
                start = part * own + head * HEAD_DIM
                raw = total[:, start : start + HEAD_DIM]
                turned = raw * cosine + pltpu.roll(raw, HEAD_DIM // 2, 1) * sine
                ref[rows, head * HEAD_DIM : (head + 1) * HEAD_DIM] = turned.astype(bf16)
        v_ref[rows, :] = total[:, 2 * own :].astype(bf16)


def head_kernel(head, q_ref, k_ref, v_ref, pos_col, seg_col, pos_row, seg_row, o_ref, token):
    token[...] = jnp.zeros_like(token)
    length = q_ref.shape[0]
    block = QUERY_BLOCK
    columns = slice(head * HEAD_DIM, (head + 1) * HEAD_DIM)

    @pl.loop(0, length // block)
    def _(i):
        rows = pl.ds(pl.multiple_of(i * block, block), block)
        allowed = visible(pos_col[rows, :], seg_col[rows, :], pos_row[...], seg_row[...])
        probs = soft_rows(q_ref[rows, columns], k_ref[:, columns], allowed)
        mixed = jnp.dot(probs.astype(bf16), v_ref[:, columns], preferred_element_type=f32)
        o_ref[rows, :] = mixed.astype(bf16)


def block_rows(ranks, count):
    ends = [0] + [(2 * step - 1) * count for step in range(1, ranks // 2 + 1)] + [ranks * count]
    return list(zip(ends[:-1], ends[1:]))


def product_blocks(source_ref, w_refs, columns, out_refs):
    start = 0
    for out_ref in out_refs:
        height, width = out_ref.shape
        depth = width // len(w_refs)
        for piece, w_ref in enumerate(w_refs):
            out_ref[:, piece * depth : (piece + 1) * depth] = lax.dot_general(
                source_ref[start : start + height, :],
                w_ref[:, columns],
                (((1,), (1,)), ((), ())),
                preferred_element_type=f32,
            ).astype(bf16)
        start += height


def branch_kernel(heads, pieces, *refs):
    o_refs = refs[:heads]
    w_refs = refs[heads : heads + pieces]
    attended_ref, *out_refs, token = refs[heads + pieces :]
    token[...] = jnp.zeros_like(token)
    own = heads * HEAD_DIM
    for head in range(heads):
        attended_ref[:, head * HEAD_DIM : (head + 1) * HEAD_DIM] = o_refs[head][...]
    product_blocks(attended_ref, w_refs, slice(3 * own, 4 * own), out_refs)


def backward_kernel(up_places, pieces, *refs):
    q_ref, k_ref, v_ref = refs[:3]
    up_blocks = refs[3 : 3 + len(up_places)]
    refs = refs[3 + len(up_places) :]
    w_refs = refs[:pieces]
    cos_ref, sin_ref, pos_col, seg_col, pos_row, seg_row = refs[pieces : 6 + pieces]
    up_ref, out_ref, *first_refs, token = refs[6 + pieces : -3]
    dk, dv, sems = refs[-3:]
    token[...] = jnp.zeros_like(token)
    copies = fetch_blocks(up_ref, up_blocks, up_places, sems)
    length, own = q_ref.shape
    depth = up_ref.shape[1] // pieces
    heads = own // HEAD_DIM
    block = QUERY_BLOCK
    scale = 1.0 / math.sqrt(HEAD_DIM)
    over_rows = (((0,), (0,)), ((), ()))
    dk[...] = jnp.zeros_like(dk)
    dv[...] = jnp.zeros_like(dv)
    for copy in copies:
        copy.wait()

    def turn_back(grad, rows):
        return grad * cos_ref[rows, :] - pltpu.roll(grad, HEAD_DIM // 2, 1) * sin_ref[rows, :]

    @pl.loop(0, length // block)
    def _(i):
        rows = pl.ds(pl.multiple_of(i * block, block), block)
        allowed = visible(pos_col[rows, :], seg_col[rows, :], pos_row[...], seg_row[...])
        total = jnp.zeros((block, own), f32)
        for piece in range(pieces):
            total = total + jnp.dot(
                up_ref[rows, piece * depth : (piece + 1) * depth],
                w_refs[piece][:, 3 * own :],
                preferred_element_type=f32,
            )
        attended_grad = total.astype(bf16)
        for head in range(heads):
            columns = slice(head * HEAD_DIM, (head + 1) * HEAD_DIM)
            query, upstream = q_ref[rows, columns], attended_grad[:, columns]
            key, value = k_ref[:, columns], v_ref[:, columns]
            probs = soft_rows(query, key, allowed)
            prob_grad = lax.dot_general(
                upstream, value, (((1,), (1,)), ((), ())), preferred_element_type=f32
            )
            inner = jnp.sum(probs * prob_grad, axis=-1, keepdims=True)
            score_grad = (probs * (prob_grad - inner)).astype(bf16)
            query_grad = jnp.dot(score_grad, key, preferred_element_type=f32) * scale
            out_ref[rows, columns] = turn_back(query_grad, rows).astype(bf16)
            dk[:, columns] += lax.dot_general(
                score_grad, query, over_rows, preferred_element_type=f32
            )
            dv[:, columns] += lax.dot_general(
                probs.astype(bf16), upstream, over_rows, preferred_element_type=f32
            )

    @pl.loop(0, length // block)
    def _(i):
        rows = pl.ds(pl.multiple_of(i * block, block), block)
        for head in range(heads):
            columns = slice(head * HEAD_DIM, (head + 1) * HEAD_DIM)
            place = slice(own + head * HEAD_DIM, own + (head + 1) * HEAD_DIM)
            out_ref[rows, place] = turn_back(dk[rows, columns] * scale, rows).astype(bf16)
        out_ref[rows, 2 * own :] = dv[rows, :].astype(bf16)

    product_blocks(out_ref, w_refs, slice(0, 3 * own), first_refs)


def attention_forward(x_blocks, weights, cosine, sine, places, blocks):
    length, width = blocks[-1][1], x_blocks[0][0].shape[1]
    own = weights[0].shape[1] // 4
    heads = own // HEAD_DIM
    piece = jax.ShapeDtypeStruct((length, own), bf16)
    whole = jax.ShapeDtypeStruct((length, width), bf16)
    zeros = jax.ShapeDtypeStruct((8, 128), f32)
    params = pltpu.CompilerParams(vmem_limit_bytes=40 * 2**20)
    x, queries, keys, values, token = pl.pallas_call(
        lambda *refs: project_kernel([place for _, *place in x_blocks], len(weights), *refs),
        out_shape=[whole] + [piece] * 3 + [zeros],
        in_specs=anywhere(len(x_blocks)) + in_vmem(len(weights) + 2),
        out_specs=in_vmem(5),
        scratch_shapes=[pltpu.SemaphoreType.DMA((len(x_blocks),))],
        compiler_params=params,
        cost_estimate=brief,
        name="project",
    )(*[array for array, *_ in x_blocks], *weights, cosine, sine)
    yield [token]
    mixed = [
        pl.pallas_call(
            lambda *refs, head=head: head_kernel(head, *refs),
            out_shape=[jax.ShapeDtypeStruct((length, HEAD_DIM), bf16), zeros],
            in_specs=in_vmem(7),
            out_specs=in_vmem(2),
            compiler_params=params,
            cost_estimate=brief,
            name="attention_head",
        )(queries, keys, values, *places)
        for head in range(heads)
    ]
    yield [token for _, token in mixed]
    attended, *branch, token = pl.pallas_call(
        lambda *refs: branch_kernel(heads, len(weights), *refs),
        out_shape=[piece]
        + [jax.ShapeDtypeStruct((end - start, width), bf16) for start, end in blocks]
        + [zeros],
        in_specs=in_vmem(heads + len(weights)),
        out_specs=in_vmem(2 + len(blocks)),
        compiler_params=params,
        cost_estimate=brief,
        name="branch",
    )(*[head for head, _ in mixed], *weights)
    yield [token]
    yield x, queries, keys, values, attended, branch


def hidden_kernel(row, x_places, y_places, pieces, fresh, *refs):
    x_blocks, refs = refs[: len(x_places)], refs[len(x_places) :]
    y_blocks, refs = refs[: len(y_places)], refs[len(y_places) :]
    w_arrays, refs = refs[:pieces], refs[pieces if fresh else pieces + 4 :]
    *wholes, second_ref, shrunk_ref, mark_ref, x_ref, y_ref, active_ref, upstream_ref = refs[:-6]
    mark_ref[...] = jnp.zeros_like(mark_ref)
    w_ref, total_ref, sems, w_sems, x_sems, y_sems = refs[-6:]
    count, width = x_ref.shape
    hidden = active_ref.shape[1]
    depth = width // pieces
    block = min(hidden, 256)
    last = (((1,), (1,)), ((), ()))
    rows_in = fetch_blocks(x_ref, x_blocks, x_places, x_sems)
    rows_in += fetch_blocks(y_ref, y_blocks, y_places, y_sems)
    fetches = [
        pltpu.make_async_copy(array, w_ref.at[piece], w_sems.at[piece])
        for piece, array in enumerate(w_arrays)
    ]
    for fetch in fetches:
        fetch.start()
    for copy in rows_in:
        copy.wait()
    copies = [
        pltpu.make_async_copy(source, whole.at[row : row + count], sems.at[index])
        for index, (source, whole) in enumerate(
            zip((x_ref, y_ref, active_ref, upstream_ref), wholes)
        )
    ]
    copies[0].start()
    copies[1].start()
    for piece, fetch in enumerate(fetches):
        fetch.wait()
        rows = slice(piece * depth, (piece + 1) * depth)
        for source, columns in (
            (x_ref, slice(0, 2 * hidden)),
            (y_ref, slice(2 * hidden, 3 * hidden)),
        ):
            term = jnp.dot(
                source[:, rows], w_ref[piece, :, columns], preferred_element_type=f32
            )
            if piece:
                total_ref[:, columns] += term
            else:
                total_ref[:, columns] = term

    @pl.loop(0, hidden // block)
    def _(i):
        columns, gates, grads = (
            pl.ds(pl.multiple_of(part * hidden + i * block, block), block) for part in range(3)
        )
        up_part, gate_part, act_grad = total_ref[:, columns], total_ref[:, gates], total_ref[:, grads]
        sigma = 1.0 / (1.0 + jnp.exp(-gate_part))
        swish = gate_part * sigma
        active_ref[:, columns] = (swish * up_part).astype(bf16)
        upstream_ref[:, columns] = (act_grad * swish).astype(bf16)
        gate_grad = act_grad * up_part * sigma * (1.0 + gate_part * (1.0 - sigma))
        upstream_ref[:, gates] = gate_grad.astype(bf16)

    copies[2].start()
    copies[3].start()
    for piece in range(pieces):
        columns = slice(piece * depth, (piece + 1) * depth)
        second_ref[:, columns] = lax.dot_general(
            upstream_ref[...], w_ref[piece, :, : 2 * hidden], last, preferred_element_type=f32
        ).astype(bf16)
        shrunk_ref[:, columns] = lax.dot_general(
            active_ref[...], w_ref[piece, :, 2 * hidden :], last, preferred_element_type=f32
        ).astype(bf16)
    for copy in copies:
        copy.wait()


def hidden_pass(row, x_blocks, y_blocks, weights, length, wholes):
    width = weights[0].shape[0] * len(weights)
    count = sum(array.size for array, *_ in x_blocks) // width
    hidden = weights[0].shape[1] // 3
    kinds = [width, width, hidden, 2 * hidden]
    fresh = not wholes
    x_places, y_places = ([place for _, *place in blocks] for blocks in (x_blocks, y_blocks))
    given = len(x_blocks) + len(y_blocks) + len(weights)
    out = pl.pallas_call(
        lambda *refs: hidden_kernel(row, x_places, y_places, len(weights), fresh, *refs),
        out_shape=[jax.ShapeDtypeStruct((length, size), bf16) for size in kinds]
        + [jax.ShapeDtypeStruct((count, width), bf16)] * 2
        + [jax.ShapeDtypeStruct((8, 128), f32)],
        in_specs=anywhere(given + len(wholes)),
        out_specs=anywhere(4) + in_vmem(3),
        scratch_shapes=[pltpu.VMEM((count, size), bf16) for size in kinds]
        + [
            pltpu.VMEM((len(weights), *weights[0].shape), bf16),
            pltpu.VMEM((count, 3 * hidden), f32),
            pltpu.SemaphoreType.DMA((4,)),
            pltpu.SemaphoreType.DMA((len(weights),)),
            pltpu.SemaphoreType.DMA((len(x_blocks),)),
            pltpu.SemaphoreType.DMA((len(y_blocks),)),
        ],
        input_output_aliases={} if fresh else {given + i: i for i in range(4)},
        compiler_params=pltpu.CompilerParams(vmem_limit_bytes=KERNEL_VMEM),
        cost_estimate=brief,
        name="hidden",
    )(*[array for array, *_ in x_blocks + y_blocks], *weights, *wholes)
    return out[:4], out[4], out[5], out[6]


def attention_backward(queries, keys, values, up_blocks, weights, cosine, sine, places, blocks):
    length, own = queries.shape
    width = up_blocks[0][0].shape[1]
    heads = own // HEAD_DIM
    return pl.pallas_call(
        lambda *refs: backward_kernel([place for _, *place in up_blocks], len(weights), *refs),
        out_shape=[
            jax.ShapeDtypeStruct((length, width), bf16),
            jax.ShapeDtypeStruct((length, 3 * own), bf16),
        ]
        + [jax.ShapeDtypeStruct((end - start, width), bf16) for start, end in blocks]
        + [jax.ShapeDtypeStruct((8, 128), f32)],
        in_specs=in_vmem(3) + anywhere(len(up_blocks)) + in_vmem(6 + len(weights)),
        out_specs=in_vmem(3 + len(blocks)),
        scratch_shapes=[
            pltpu.VMEM((length, own), f32),
            pltpu.VMEM((length, own), f32),
            pltpu.SemaphoreType.DMA((len(up_blocks),)),
        ],
        compiler_params=pltpu.CompilerParams(vmem_limit_bytes=KERNEL_VMEM),
        cost_estimate=brief,
        name="attention_backward",
    )(
        queries,
        keys,
        values,
        *[array for array, *_ in up_blocks],
        *weights,
        cosine,
        sine,
        *places,
    )


def normed_rows(values):
    centered = values - jnp.mean(values, axis=-1, keepdims=True)
    inverse = lax.rsqrt(jnp.mean(centered * centered, axis=-1, keepdims=True) + norm_epsilon)
    return centered * inverse, inverse


def norm_back_rows(values, upstream):
    normed, inverse = normed_rows(values)
    return inverse * (
        upstream
        - jnp.mean(upstream, axis=-1, keepdims=True)
        - normed * jnp.mean(upstream * normed, axis=-1, keepdims=True)
    )


def row_call(kernel, name, kinds, *arrays, waits=()):
    shape = arrays[0].shape

    def run(*refs):
        refs[-1][...] = jnp.zeros_like(refs[-1])
        kernel(*refs[: len(arrays)], *refs[len(arrays) + len(waits) : -1])

    return pl.pallas_call(
        run,
        out_shape=[jax.ShapeDtypeStruct(shape, kind) for kind in kinds]
        + [jax.ShapeDtypeStruct((8, 128), f32)],
        in_specs=in_vmem(len(arrays)) + anywhere(len(waits)),
        out_specs=in_vmem(len(kinds) + 1),
        compiler_params=pltpu.CompilerParams(vmem_limit_bytes=KERNEL_VMEM),
        name=name,
    )(*arrays, *waits)


def wide(*refs):
    total = refs[0][...].astype(f32)
    for ref in refs[1:]:
        total = total + ref[...].astype(f32)
    return total


def join_kernel(token_ref, own_ref, up0, down0, up1, down1, residual_ref, norm_ref):
    middle = own_ref.shape[1] // 2
    for columns, refs in ((slice(0, middle), (up0, down0)), (slice(middle, None), (up1, down1))):
        residual_ref[:, columns] = token_ref[:, columns].astype(f32) + (
            own_ref[:, columns].astype(f32) + wide(*refs)
        )
    norm_ref[...] = normed_rows(residual_ref[...])[0].astype(bf16)


def turn_kernel(residual_ref, back_ref, own_ref, up0, down0, up1, down1, grad_ref, low_ref):
    upstream = own_ref[...].astype(f32) + jnp.concatenate([wide(up0, down0), wide(up1, down1)], 1)
    grad = back_ref[...].astype(f32) + norm_back_rows(residual_ref[...], upstream)
    grad_ref[...] = grad
    low_ref[...] = grad.astype(bf16)


def last_kernel(token_ref, grad_ref, residual_ref, own0, up0, down0, own1, up1, down1, in_ref, out_ref):
    in_ref[...] = grad_ref[...] + norm_back_rows(token_ref[...].astype(f32), wide(own0, up0, down0))
    out_ref[...] = (residual_ref[...] + wide(own1, up1, down1)).astype(bf16)


def weight_term(shards, k, products, adds=(), waits=(), cuts=1):
    length, width = products[0][0].shape
    depth = width // shards
    block = min(right.shape[1] for _, right in products)
    steps = [right.shape[1] // block for _, right in products]
    firsts = [sum(steps[:i]) for i in range(len(steps))]
    height = depth // cuts
    places = [(row, array.shape[0]) for array, row in adds]
    spans = places or [(i * height, height) for i in range(cuts)]

    def kernel(*refs):
        *outs, token = refs[-1 - cuts :]
        more = refs[2 * len(products) : 2 * len(products) + len(adds)]
        step = pl.program_id(0)
        token[...] = jnp.zeros_like(token)
        for index, first in enumerate(firsts):

            @pl.when((step >= first) & (step < first + steps[index]))
            def _():
                total = lax.dot_general(
                    refs[2 * index][...],
                    refs[2 * index + 1][...],
                    (((0,), (0,)), ((), ())),
                    preferred_element_type=f32,
                )
                for number, (row, rows) in enumerate(spans):
                    piece = total[row : row + rows]
                    if more:
                        piece = piece + more[number][...].astype(f32)
                    place = row % height
                    outs[row // height][place : place + rows, :] = piece.astype(bf16)

    specs, arrays = [], []
    for (left, right), first, size in zip(products, firsts, steps):
        specs.append(pl.BlockSpec((length, depth), lambda n: (0, k)))
        specs.append(
            pl.BlockSpec(
                (length, block),
                lambda n, first=first, size=size: (0, jnp.clip(n - first, 0, size - 1)),
            )
        )
        arrays += [left, right]
    return pl.pallas_call(
        kernel,
        grid=(sum(steps),),
        out_shape=[jax.ShapeDtypeStruct((height, sum(steps) * block), bf16)] * cuts
        + [jax.ShapeDtypeStruct((8, 128), f32)],
        in_specs=specs
        + [pl.BlockSpec((rows, block), lambda n: (0, n)) for _, rows in places]
        + anywhere(len(waits)),
        out_specs=[pl.BlockSpec((height, block), lambda n: (0, n))] * cuts
        + [pl.BlockSpec((8, 128), lambda n: (0, 0))],
        compiler_params=pltpu.CompilerParams(vmem_limit_bytes=KERNEL_VMEM),
        cost_estimate=brief,
        name="weight_term",
    )(*arrays, *[array for array, _ in adds], *waits)


def adam_kernel(rate, factor_ref, w_ref, m_ref, v_ref, g_ref, w_out, m_out, v_out):
    ranks, _, block = g_ref.shape
    for rank in range(ranks):
        columns = slice(rank * block, (rank + 1) * block)
        w_out[:, columns], m_out[:, columns], v_out[:, columns] = adam_update(
            w_ref[:, columns],
            m_ref[:, columns],
            v_ref[:, columns],
            g_ref[rank].astype(f32),
            factor_ref[0, 0],
            rate,
        )


def adam_step(weight, mean, square, grad, first, groups, factor, rate):
    ranks, rows, _ = grad.shape
    block = weight.shape[1] // (groups * ranks)
    held = max(1, min(ranks, ADAM_COLUMNS // block))
    steps = ranks // held
    flat = pl.BlockSpec((rows, held * block), lambda g, r: (0, g * steps + r))
    shape = jax.ShapeDtypeStruct(weight.shape, f32)
    return pl.pallas_call(
        lambda *refs: adam_kernel(rate, *refs),
        grid=(groups, steps),
        out_shape=[shape] * 3,
        in_specs=[
            pl.BlockSpec(memory_space=pltpu.SMEM),
            flat,
            flat,
            flat,
            pl.BlockSpec((held, rows, block), lambda g, r: (r, 0, first + g)),
        ],
        out_specs=[flat] * 3,
        compiler_params=pltpu.CompilerParams(vmem_limit_bytes=KERNEL_VMEM),
        cost_estimate=brief,
        name="adam_step",
    )(factor.reshape(1, 1), weight, mean, square, grad)


def body(ranks, shards):
    def run(
        tokens,
        cotangent,
        positions,
        segments,
        joint_weight,
        joint_mean,
        joint_square,
        output_weight,
        output_mean,
        output_square,
        expand_weight,
        expand_mean,
        expand_square,
        shrink_weight,
        shrink_mean,
        shrink_square,
    ):
        shard = lax.axis_index("fsdp")
        count, width = tokens.shape[1], tokens.shape[2]
        hidden = shrink_weight.shape[1]
        own = width // ranks
        own_hidden = hidden // ranks
        rows = width // (ranks * shards)
        y_rows = shards // CORES
        near_table = [
            [((f // CORES + k // CORES) % y_rows) * CORES + (f % CORES ^ k % CORES) for k in range(shards)]
            for f in range(shards)
        ]
        back_table = [[row.index(f) for f in range(shards)] for row in near_table]
        chunk_of = lax.dynamic_index_in_dim(jnp.array(near_table, jnp.int32), shard, 0, False)
        chunk_back = lax.dynamic_index_in_dim(jnp.array(back_table, jnp.int32), shard, 0, False)

        def to_inner(values):
            split = values.reshape(count, ranks, shards, rows).transpose(2, 0, 1, 3)
            return jnp.take(split, chunk_of, axis=0).transpose(1, 0, 2, 3).reshape(count, width)

        def to_outer(values):
            split = values.reshape(count, shards, ranks, rows).transpose(1, 0, 2, 3)
            return jnp.take(split, chunk_back, axis=0).transpose(1, 2, 0, 3).reshape(count, width)

        def columns_of(weight, groups):
            split = weight.astype(bf16).reshape(rows, groups, ranks, -1).transpose(2, 0, 1, 3)
            return split.reshape(ranks * rows, -1)

        def exchange(split):
            moved = lax.all_to_all(split.reshape(ranks, rows, -1), "ctx", 0, 0, tiled=True)
            return moved.reshape(ranks * rows, -1)

        def by_rank(moved):
            return moved.reshape(ranks, rows, -1)

        ahead, back = y_perm(shards, 1), y_perm(shards, -1)
        swap = core_perm(shards)

        def swapped(value):
            return lax.ppermute(value, "fsdp", swap)

        def across_y(block):
            blocks = [block]
            for _ in range(y_rows - 1):
                blocks.append(lax.ppermute(blocks[-1], "fsdp", back))
            return blocks

        def with_cores(blocks):
            return [piece for block in blocks for piece in (block, swapped(block))]

        token_low = to_inner(tokens[0])
        back_low = to_inner(cotangent[0])
        joint_split = columns_of(joint_weight, 3)
        output_split = columns_of(output_weight, 1)
        near_moved = exchange(jnp.concatenate([joint_split, output_split], 1))
        far_split = jnp.concatenate([columns_of(expand_weight, 2), columns_of(shrink_weight, 1)], 1)
        near_moved, far_split = hold(near_moved, far_split)
        far_moved = exchange(far_split)
        near_blocks = across_y(near_moved)

        order = ring_order(ranks)
        block_table = [
            [order[(order.index(i) + d) % ranks] for d in pair_order(ranks)] for i in range(ranks)
        ]
        block_of = lax.dynamic_index_in_dim(
            jnp.array(block_table, jnp.int32), lax.axis_index("ctx"), 0, False
        )
        pos = jnp.take(positions[0].reshape(ranks, count), block_of, axis=0).reshape(-1)
        seg = jnp.take(segments[0].reshape(ranks, count), block_of, axis=0).reshape(-1)
        places = (pos[:, None], seg[:, None], pos[None, :], seg[None, :])
        turn = HEAD_DIM // 2
        inverse = jnp.exp(jnp.arange(turn).astype(f32) * (-2.0 * math.log(rope_base) / HEAD_DIM))
        angles = pos.astype(f32)[:, None] * inverse[None, :]
        cosine, sine = jnp.cos(angles), jnp.sin(angles)
        cosine = jnp.concatenate([cosine, cosine], 1)
        sine = jnp.concatenate([-sine, sine], 1)

        def collect(products):
            total = None
            waits = yield
            for step in range(y_rows - 1, -1, -1):
                *terms, token = weight_term(shards, step * CORES + 1, products, (), waits, 4)
                adds = [(swapped(term), i * term.shape[0]) for i, term in enumerate(terms)]
                waits = yield token
                term, token = weight_term(shards, step * CORES, products, adds, waits)
                if step == 0:
                    yield token
                if total is not None:
                    term = (term.astype(f32) + total.astype(f32)).astype(bf16)
                if step:
                    total = lax.ppermute(term, "fsdp", ahead)
                    waits = yield token
            yield term

        def finish(work):
            result = None
            while True:
                try:
                    result = work.send([])
                except StopIteration:
                    return result

        def collect_all(products):
            work = collect(products)
            next(work)
            return finish(work)

        def square_sum(grad):
            return jnp.sum(jnp.square(grad.astype(f32)))

        first_own = layer_norm(token_low.astype(f32)).astype(bf16)
        first_own, far_moved, back_low, *near_blocks[1:] = hold(
            first_own, far_moved, back_low, *near_blocks[1:]
        )
        near = with_cores(near_blocks)
        far_blocks = across_y(far_moved)
        first_blocks = ring_gather(first_own, ranks, 2)
        near_core = swapped(far_moved)
        first_blocks, (back_low, near_core) = hold_ends(first_blocks, back_low, near_core)
        blocks = block_rows(ranks, count)
        work = attention_forward(flat(first_blocks), near, cosine, sine, places, blocks)
        back_blocks = ring_gather(
            back_low, ranks, beside=lambda step: next(work) if step <= 3 else []
        )
        first_norm, queries, keys, values, attended, branch = list(work)[-1]
        middle = width // 2
        branch_sides = (branch, 0, middle), (branch, middle, width)
        sends = first_sends(*branch_sides)
        back_blocks, held = hold_ends(back_blocks, *sends, *far_blocks[1:])
        sends, far_blocks[1:] = held[:4], held[4:]
        cores = [near_core] + [swapped(block) for block in far_blocks[1:]]
        far = [piece for pair in zip(far_blocks, cores) for piece in pair]
        sums = twin_scatter(
            *branch_sides, sends, ranks, lambda turn, _: cores[1:] if turn == 2 else []
        )
        residual, second_own, _ = row_call(
            join_kernel, "join", (f32, bf16), token_low, branch[0], *sums[0], *sums[1]
        )

        half = ranks // 2
        length = ranks * count
        wholes, terms, shrunk = [], [None] * (half + 1), [None] * (half + 1)

        def pass_rows(step, x_blocks, y_blocks):
            first = x_blocks[0][1] if step < half else 0
            far_row = (ranks - 1) * count

            def local(given):
                return [
                    (array, count if step == half and row == far_row else row - first, column)
                    for array, row, column in given
                ]

            start = 2 * (step - 1) * count
            wholes[:], second, out, mark = hidden_pass(
                start, local(x_blocks), local(y_blocks), far, length, list(wholes)
            )
            if step < half:
                terms[step], shrunk[step] = second, out
            else:
                terms[0], terms[half] = second[:count], second[count:]
                shrunk[0], shrunk[half] = out[:count], out[count:]
            return [mark]

        def arrived(step, x_blocks):
            return pass_rows(step, x_blocks, back_blocks[step % half])

        ring_gather(second_own, ranks, 1, arrived)
        second_norm, back_rows, activated, upstream = wholes
        shrink_work = collect([(back_rows, activated)])
        expand_work = collect([(second_norm, upstream)])
        next(shrink_work), next(expand_work)

        def first_half(turn, tokens):
            return [shrink_work.send([tokens[turn - 2]])] if turn in (2, 4) and y_rows > 1 else []

        term_sides = (terms, 0, middle), (terms, middle, width)
        sums = twin_scatter(*term_sides, first_sends(*term_sides), ranks, first_half)
        residual_grad, branch_low, mark = row_call(
            turn_kernel, "turn", (f32, bf16), residual, back_low, terms[0], *sums[0], *sums[1]
        )

        def second_half(step):
            if y_rows == 1 or step > 3:
                return []
            work = [expand_work, shrink_work] if step == 1 else [expand_work]
            return [one.send([mark]) for one in work]

        branch_blocks = ring_gather(branch_low, ranks, beside=second_half)
        branch_blocks, (shrink_grad, _) = hold_ends(
            branch_blocks, finish(shrink_work), expand_work.send([])
        )
        shrink_back = exchange(shrink_grad)
        branch_grad, joint_upstream, *first_part, mark = attention_backward(
            queries, keys, values, flat(branch_blocks), near, cosine, sine, places, blocks
        )
        expand_grad, shrink_back, _ = hold(finish(expand_work), shrink_back, mark)
        expand_back = exchange(expand_grad)
        near_grad = collect_all([(first_norm, joint_upstream), (branch_grad, attended)])
        near_grad, expand_back = hold(near_grad, expand_back)
        near_back = exchange(near_grad)
        squares = square_sum(near_back) + square_sum(shrink_back) + square_sum(expand_back)
        total = sum_everywhere(squares, ranks, shards)
        last_sides = (first_part, 0, width), (shrunk, 0, width)
        *sends, near_back = hold(*first_sends(*last_sides), near_back)
        grad_norm = jnp.sqrt(total[0, 0])
        factor = jnp.minimum(1.0, clip_limit / (grad_norm + 1e-06))
        joint_new = adam_step(
            joint_weight, joint_mean, joint_square, by_rank(near_back), 0, 3, factor, main_rate
        )
        output_new = adam_step(
            output_weight, output_mean, output_square, by_rank(near_back), 3, 1, factor, output_rate
        )
        expand_new = adam_step(
            expand_weight, expand_mean, expand_square, by_rank(expand_back), 0, 2, factor, main_rate
        )
        shrink_new = adam_step(
            shrink_weight, shrink_mean, shrink_square, by_rank(shrink_back), 0, 1, factor, main_rate
        )
        sums = twin_scatter(
            *last_sides,
            sends,
            ranks,
            lambda turn, _: {0: [total], 2: joint_new + output_new, 3: shrink_new}.get(turn, []),
        )
        input_inner, layer_inner, _ = row_call(
            last_kernel,
            "last",
            (f32, bf16),
            token_low,
            residual_grad,
            residual,
            first_part[0],
            *sums[0],
            shrunk[0],
            *sums[1],
            waits=expand_new[:1],
        )
        input_grad = to_outer(input_inner)[None]
        layer_output = to_outer(layer_inner)[None]
        return (
            layer_output,
            input_grad,
            grad_norm,
            *joint_new,
            *output_new,
            *expand_new,
            *shrink_new,
        )

    return run


def solution(mesh):
    tokens_spec = P("fsdp", "ctx", None)
    place_spec = P("fsdp", None)
    weight_spec = P(("ctx", "fsdp"), None)
    return jax.shard_map(
        body(mesh.shape["ctx"], mesh.shape["fsdp"]),
        mesh=mesh,
        in_specs=(tokens_spec, tokens_spec, place_spec, place_spec) + (weight_spec,) * 12,
        out_specs=(tokens_spec, tokens_spec, P()) + (weight_spec,) * 12,
        check_vma=False,
    )
```

```python
import math

import jax
import jax.numpy as jnp
from jax import lax
from jax.experimental import pallas as pl
from jax.experimental.pallas import tpu as pltpu
from jax.sharding import PartitionSpec as P

HEAD_DIM = 128
STEP = 10
LINE = 4
CORES = 2
QUERY_BLOCK = 256
ADAM_COLUMNS = 2048
KERNEL_VMEM = 60 * 2**20

norm_epsilon = 1e-05
rope_base = 10000.0
clip_limit = 1.0
beta_first = 0.9
beta_second = 0.95
adam_epsilon = 1e-08
decay_rate = 0.1
main_rate = 0.02
output_rate = 0.2
masked_score = -1e30

f32 = jnp.float32
bf16 = jnp.bfloat16


def layer_norm(values):
    centered = values - jnp.mean(values, axis=-1, keepdims=True)
    return centered * lax.rsqrt(
        jnp.mean(centered * centered, axis=-1, keepdims=True) + norm_epsilon
    )


def adam_update(weight, moment_one, moment_two, gradient, factor, step_rate):
    clipped = gradient * factor
    mean_new = beta_first * moment_one + (1.0 - beta_first) * clipped
    square_new = beta_second * moment_two + (1.0 - beta_second) * clipped * clipped
    mean_hat = mean_new / (1.0 - beta_first**STEP)
    square_hat = square_new / (1.0 - beta_second**STEP)
    weight_new = weight - step_rate * (
        mean_hat / (jnp.sqrt(square_hat) + adam_epsilon) + decay_rate * weight
    )
    return (weight_new, mean_new, square_new)


def ring_order(ranks):
    lines = ranks // LINE
    order = []
    for x in range(lines):
        places = range(LINE) if x % 2 == 0 else range(LINE - 1, -1, -1)
        order += [z * lines + x for z in places]
    return order


def ring_perms(ranks):
    order = ring_order(ranks)
    right = [(order[i], order[(i + 1) % ranks]) for i in range(ranks)]
    return right, [(b, a) for a, b in right]


brief = pl.CostEstimate(flops=10**6, bytes_accessed=10**5, transcendentals=0)


def anywhere(count):
    return [pl.BlockSpec(memory_space=pl.ANY)] * count


def in_vmem(count):
    return [pl.BlockSpec(memory_space=pltpu.VMEM)] * count


def like(values):
    return [jax.ShapeDtypeStruct(value.shape, value.dtype) for value in values]


def hold(*values):
    return pl.pallas_call(
        lambda *refs: None,
        out_shape=like(values),
        in_specs=anywhere(len(values)),
        out_specs=anywhere(len(values)),
        input_output_aliases={i: i for i in range(len(values))},
        name="hold",
    )(*values)


def pair_order(ranks):
    half = ranks // 2
    return [0] + [d for step in range(1, half) for d in (-step, step)] + [half]


def ring_gather(block, ranks, parts=1, arrived=None, beside=None, mark=()):
    right, left = ring_perms(ranks)
    half = ranks // 2
    count, width = block.shape
    middle = width // 2
    size = width // parts
    up = [block[:, i * size : (i + 1) * size] for i in range(parts)]
    down = list(up)
    lists = []
    for step in range(1, half):
        row = (2 * step - 1) * count
        lists.append([])
        for i in range(parts):
            up[i] = lax.ppermute(up[i], "ctx", right)
            down[i] = lax.ppermute(down[i], "ctx", left)
            lists[-1] += [(up[i], row, i * size), (down[i], row + count, i * size)]
        if parts == 1:
            also = beside(step) if beside else mark
            up[0], down[0], *_ = hold(up[0], down[0], *also)
            lists[-1] = [(up[0], row, 0), (down[0], row + count, 0)]
        if arrived:
            mark = arrived(step, lists[-1])
    first = up[0] if parts == 2 else up[0][:, :middle]
    last = down[1] if parts == 2 else down[0][:, middle:]
    first = lax.ppermute(first, "ctx", right)
    last = lax.ppermute(last, "ctx", left)
    row = (ranks - 1) * count
    ends = [(block, 0, 0), (first, row, 0), (last, row, middle)]
    if arrived:
        arrived(half, ends)
    return [ends] + lists


def flat(lists):
    return [block for blocks in lists for block in blocks]


def hold_ends(lists, *others):
    ends = lists[0][1:] + lists[-1]
    held = hold(*[array for array, *_ in ends], *others)
    ends = [(array, *place) for array, (_, *place) in zip(held, ends)]
    lists = [[lists[0][0]] + ends[:2]] + lists[1:-1] + [ends[2:]]
    return lists, held[len(ends) :]


def fetch_blocks(target, refs, places, sems):
    copies = []
    for index, (ref, (row, column)) in enumerate(zip(refs, places)):
        height, width = ref.shape
        place = target.at[row : row + height, column : column + width]
        copies.append(pltpu.make_async_copy(ref, place, sems.at[index]))
        copies[-1].start()
    return copies


def scatter_tick(up, down, up_part, down_part, waits):
    count = up.shape[0]
    parts = (up_part, down_part)
    sends = [jax.ShapeDtypeStruct((count, end - start), bf16) for _, _, start, end in parts]

    def kernel(*refs):
        up_out, down_out, token = refs[-3:]
        for ref, pair_ref, out, row, (_, column, start, end) in (
            (refs[0], refs[2], up_out, count, up_part),
            (refs[1], refs[3], down_out, 0, down_part),
        ):
            size = ref.shape[1]
            if size < end - start:
                out[...] = pair_ref[row : row + count, start:end]
            own = pair_ref[row : row + count, column : column + size]
            out[:, column - start : column - start + size] = (
                ref[...].astype(f32) + own.astype(f32)
            ).astype(bf16)
        token[...] = jnp.zeros_like(token)

    return pl.pallas_call(
        kernel,
        out_shape=sends + [jax.ShapeDtypeStruct((8, 128), f32)],
        in_specs=in_vmem(4) + anywhere(len(waits)),
        out_specs=in_vmem(3),
        compiler_params=pltpu.CompilerParams(vmem_limit_bytes=KERNEL_VMEM),
        name="scatter_tick",
    )(up, down, up_part[0], down_part[0], *waits)


class Scatter:
    def __init__(self, ranks, waits):
        self.right, self.left = ring_perms(ranks)
        self.waits, self.tokens = waits, []

    def send(self, up, down):
        return lax.ppermute(up, "ctx", self.right), lax.ppermute(down, "ctx", self.left)

    def add(self, state, up_part, down_part):
        turn = len(self.tokens)
        waiting = self.tokens[-1:] + list(self.waits(turn, self.tokens))
        up, down, token = scatter_tick(*state, up_part, down_part, waiting)
        self.tokens.append(token)
        return self.send(up, down)


def first_sends(low, high):
    half = len(low[0]) - 1
    count = low[0][0].shape[0]

    def columns(side, step):
        blocks, start, end = side
        return blocks[step][:, start:end]

    return [
        columns(low, half),
        columns(high, half),
        columns(high, half - 1)[count:],
        columns(low, half - 1)[:count],
    ]


def twin_scatter(low, high, sends, ranks, waits=lambda turn, tokens: []):
    ring = Scatter(ranks, waits)

    def part(side, step):
        blocks, start, end = side
        return (blocks[step], start, start, end)

    first = ring.send(sends[0], sends[1])
    second = ring.send(sends[2], sends[3])
    for step in range(ranks // 2 - 1, 0, -1):
        first = ring.add(first, part(low, step), part(high, step))
        if step > 1:
            second = ring.add(second, part(high, step - 1), part(low, step - 1))
    return (first[0], second[1]), (second[0], first[1])


def sum_everywhere(value, ranks, shards):
    held = jnp.full((8, 128), value, f32)
    for axis, size in (("fsdp", shards), ("ctx", ranks)):
        step = 1
        while step < size:
            held = held + lax.ppermute(held, axis, [(i, i ^ step) for i in range(size)])
            step *= 2
    return held


def core_perm(shards):
    return [(i, i ^ 1) for i in range(shards)]


def y_perm(shards, step):
    rows = shards // CORES
    return [(i, ((i // CORES + step) % rows) * CORES + i % CORES) for i in range(shards)]


def visible(pos_col, seg_col, pos_row, seg_row):
    return (seg_col == seg_row) & (pos_row <= pos_col)


def soft_rows(query, key, allowed):
    score = lax.dot_general(query, key, (((1,), (1,)), ((), ())), preferred_element_type=f32)
    masked = jnp.where(allowed, score * (1.0 / math.sqrt(HEAD_DIM)), masked_score)
    top = jnp.max(masked, axis=-1, keepdims=True)
    exponent = jnp.exp(masked - top)
    return exponent * (1.0 / jnp.sum(exponent, axis=-1, keepdims=True))


def project_kernel(places, pieces, *refs):
    blocks = refs[: len(places)]
    w_refs = refs[len(places) : len(places) + pieces]
    cos_ref, sin_ref, x_ref, q_ref, k_ref, v_ref, token, sems = refs[len(places) + pieces :]
    token[...] = jnp.zeros_like(token)
    length = x_ref.shape[0]
    depth = x_ref.shape[1] // pieces
    own = q_ref.shape[1]
    block = QUERY_BLOCK
    for copy in fetch_blocks(x_ref, blocks, places, sems):
        copy.wait()

    @pl.loop(0, length // block)
    def _(i):
        rows = pl.ds(pl.multiple_of(i * block, block), block)
        total = jnp.zeros((block, 3 * own), f32)
        for piece in range(pieces):
            total = total + jnp.dot(
                x_ref[rows, piece * depth : (piece + 1) * depth],
                w_refs[piece][:, : 3 * own],
                preferred_element_type=f32,
            )
        cosine, sine = cos_ref[rows, :], sin_ref[rows, :]
        for part, ref in ((0, q_ref), (1, k_ref)):
            for head in range(own // HEAD_DIM):
                start = part * own + head * HEAD_DIM
                raw = total[:, start : start + HEAD_DIM]
                turned = raw * cosine + pltpu.roll(raw, HEAD_DIM // 2, 1) * sine
                ref[rows, head * HEAD_DIM : (head + 1) * HEAD_DIM] = turned.astype(bf16)
        v_ref[rows, :] = total[:, 2 * own :].astype(bf16)


def head_kernel(head, q_ref, k_ref, v_ref, pos_col, seg_col, pos_row, seg_row, o_ref, token):
    token[...] = jnp.zeros_like(token)
    length = q_ref.shape[0]
    block = QUERY_BLOCK
    columns = slice(head * HEAD_DIM, (head + 1) * HEAD_DIM)

    @pl.loop(0, length // block)
    def _(i):
        rows = pl.ds(pl.multiple_of(i * block, block), block)
        allowed = visible(pos_col[rows, :], seg_col[rows, :], pos_row[...], seg_row[...])
        probs = soft_rows(q_ref[rows, columns], k_ref[:, columns], allowed)
        mixed = jnp.dot(probs.astype(bf16), v_ref[:, columns], preferred_element_type=f32)
        o_ref[rows, :] = mixed.astype(bf16)


def block_rows(ranks, count):
    ends = [0] + [(2 * step - 1) * count for step in range(1, ranks // 2 + 1)] + [ranks * count]
    return list(zip(ends[:-1], ends[1:]))


def product_blocks(source_ref, w_refs, columns, out_refs):
    start = 0
    for out_ref in out_refs:
        height, width = out_ref.shape
        depth = width // len(w_refs)
        for piece, w_ref in enumerate(w_refs):
            out_ref[:, piece * depth : (piece + 1) * depth] = lax.dot_general(
                source_ref[start : start + height, :],
                w_ref[:, columns],
                (((1,), (1,)), ((), ())),
                preferred_element_type=f32,
            ).astype(bf16)
        start += height


def branch_kernel(heads, pieces, *refs):
    o_refs = refs[:heads]
    w_refs = refs[heads : heads + pieces]
    attended_ref, *out_refs, token = refs[heads + pieces :]
    token[...] = jnp.zeros_like(token)
    own = heads * HEAD_DIM
    for head in range(heads):
        attended_ref[:, head * HEAD_DIM : (head + 1) * HEAD_DIM] = o_refs[head][...]
    product_blocks(attended_ref, w_refs, slice(3 * own, 4 * own), out_refs)


def backward_kernel(up_places, pieces, *refs):
    q_ref, k_ref, v_ref = refs[:3]
    up_blocks = refs[3 : 3 + len(up_places)]
    refs = refs[3 + len(up_places) :]
    w_refs = refs[:pieces]
    cos_ref, sin_ref, pos_col, seg_col, pos_row, seg_row = refs[pieces : 6 + pieces]
    up_ref, out_ref, *first_refs, token = refs[6 + pieces : -3]
    dk, dv, sems = refs[-3:]
    token[...] = jnp.zeros_like(token)
    copies = fetch_blocks(up_ref, up_blocks, up_places, sems)
    length, own = q_ref.shape
    depth = up_ref.shape[1] // pieces
    heads = own // HEAD_DIM
    block = QUERY_BLOCK
    scale = 1.0 / math.sqrt(HEAD_DIM)
    over_rows = (((0,), (0,)), ((), ()))
    dk[...] = jnp.zeros_like(dk)
    dv[...] = jnp.zeros_like(dv)
    for copy in copies:
        copy.wait()

    def turn_back(grad, rows):
        return grad * cos_ref[rows, :] - pltpu.roll(grad, HEAD_DIM // 2, 1) * sin_ref[rows, :]

    @pl.loop(0, length // block)
    def _(i):
        rows = pl.ds(pl.multiple_of(i * block, block), block)
        allowed = visible(pos_col[rows, :], seg_col[rows, :], pos_row[...], seg_row[...])
        total = jnp.zeros((block, own), f32)
        for piece in range(pieces):
            total = total + jnp.dot(
                up_ref[rows, piece * depth : (piece + 1) * depth],
                w_refs[piece][:, 3 * own :],
                preferred_element_type=f32,
            )
        attended_grad = total.astype(bf16)
        for head in range(heads):
            columns = slice(head * HEAD_DIM, (head + 1) * HEAD_DIM)
            query, upstream = q_ref[rows, columns], attended_grad[:, columns]
            key, value = k_ref[:, columns], v_ref[:, columns]
            probs = soft_rows(query, key, allowed)
            prob_grad = lax.dot_general(
                upstream, value, (((1,), (1,)), ((), ())), preferred_element_type=f32
            )
            inner = jnp.sum(probs * prob_grad, axis=-1, keepdims=True)
            score_grad = (probs * (prob_grad - inner)).astype(bf16)
            query_grad = jnp.dot(score_grad, key, preferred_element_type=f32) * scale
            out_ref[rows, columns] = turn_back(query_grad, rows).astype(bf16)
            dk[:, columns] += lax.dot_general(
                score_grad, query, over_rows, preferred_element_type=f32
            )
            dv[:, columns] += lax.dot_general(
                probs.astype(bf16), upstream, over_rows, preferred_element_type=f32
            )

    @pl.loop(0, length // block)
    def _(i):
        rows = pl.ds(pl.multiple_of(i * block, block), block)
        for head in range(heads):
            columns = slice(head * HEAD_DIM, (head + 1) * HEAD_DIM)
            place = slice(own + head * HEAD_DIM, own + (head + 1) * HEAD_DIM)
            out_ref[rows, place] = turn_back(dk[rows, columns] * scale, rows).astype(bf16)
        out_ref[rows, 2 * own :] = dv[rows, :].astype(bf16)

    product_blocks(out_ref, w_refs, slice(0, 3 * own), first_refs)


def attention_forward(x_blocks, weights, cosine, sine, places, blocks):
    length, width = blocks[-1][1], x_blocks[0][0].shape[1]
    own = weights[0].shape[1] // 4
    heads = own // HEAD_DIM
    piece = jax.ShapeDtypeStruct((length, own), bf16)
    whole = jax.ShapeDtypeStruct((length, width), bf16)
    zeros = jax.ShapeDtypeStruct((8, 128), f32)
    params = pltpu.CompilerParams(vmem_limit_bytes=KERNEL_VMEM)
    x, queries, keys, values, token = pl.pallas_call(
        lambda *refs: project_kernel([place for _, *place in x_blocks], len(weights), *refs),
        out_shape=[whole] + [piece] * 3 + [zeros],
        in_specs=anywhere(len(x_blocks)) + in_vmem(len(weights) + 2),
        out_specs=in_vmem(5),
        scratch_shapes=[pltpu.SemaphoreType.DMA((len(x_blocks),))],
        compiler_params=params,
        cost_estimate=brief,
        name="project",
    )(*[array for array, *_ in x_blocks], *weights, cosine, sine)
    yield [token]
    mixed = [
        pl.pallas_call(
            lambda *refs, head=head: head_kernel(head, *refs),
            out_shape=[jax.ShapeDtypeStruct((length, HEAD_DIM), bf16), zeros],
            in_specs=in_vmem(7),
            out_specs=in_vmem(2),
            compiler_params=params,
            cost_estimate=brief,
            name="attention_head",
        )(queries, keys, values, *places)
        for head in range(heads)
    ]
    yield [token for _, token in mixed]
    attended, *branch, token = pl.pallas_call(
        lambda *refs: branch_kernel(heads, len(weights), *refs),
        out_shape=[piece]
        + [jax.ShapeDtypeStruct((end - start, width), bf16) for start, end in blocks]
        + [zeros],
        in_specs=in_vmem(heads + len(weights)),
        out_specs=in_vmem(2 + len(blocks)),
        compiler_params=params,
        cost_estimate=brief,
        name="branch",
    )(*[head for head, _ in mixed], *weights)
    yield [token]
    yield x, queries, keys, values, attended, branch


def hidden_kernel(row, x_places, y_places, pieces, fresh, *refs):
    x_blocks, refs = refs[: len(x_places)], refs[len(x_places) :]
    y_blocks, refs = refs[: len(y_places)], refs[len(y_places) :]
    w_arrays, refs = refs[:pieces], refs[pieces if fresh else pieces + 4 :]
    *wholes, second_ref, shrunk_ref, mark_ref, x_ref, y_ref, active_ref, upstream_ref = refs[:-6]
    mark_ref[...] = jnp.zeros_like(mark_ref)
    w_ref, total_ref, sems, w_sems, x_sems, y_sems = refs[-6:]
    count, width = x_ref.shape
    hidden = active_ref.shape[1]
    depth = width // pieces
    block = min(hidden, 256)
    last = (((1,), (1,)), ((), ()))
    rows_in = fetch_blocks(x_ref, x_blocks, x_places, x_sems)
    rows_in += fetch_blocks(y_ref, y_blocks, y_places, y_sems)
    fetches = [
        pltpu.make_async_copy(array, w_ref.at[piece], w_sems.at[piece])
        for piece, array in enumerate(w_arrays)
    ]
    for fetch in fetches:
        fetch.start()
    for copy in rows_in:
        copy.wait()
    copies = [
        pltpu.make_async_copy(source, whole.at[row : row + count], sems.at[index])
        for index, (source, whole) in enumerate(
            zip((x_ref, y_ref, active_ref, upstream_ref), wholes)
        )
    ]
    copies[0].start()
    copies[1].start()
    for piece, fetch in enumerate(fetches):
        fetch.wait()
        rows = slice(piece * depth, (piece + 1) * depth)
        for source, columns in (
            (x_ref, slice(0, 2 * hidden)),
            (y_ref, slice(2 * hidden, 3 * hidden)),
        ):
            term = jnp.dot(
                source[:, rows], w_ref[piece, :, columns], preferred_element_type=f32
            )
            if piece:
                total_ref[:, columns] += term
            else:
                total_ref[:, columns] = term

    @pl.loop(0, hidden // block)
    def _(i):
        columns, gates, grads = (
            pl.ds(pl.multiple_of(part * hidden + i * block, block), block) for part in range(3)
        )
        up_part, gate_part, act_grad = total_ref[:, columns], total_ref[:, gates], total_ref[:, grads]
        sigma = 1.0 / (1.0 + jnp.exp(-gate_part))
        swish = gate_part * sigma
        active_ref[:, columns] = (swish * up_part).astype(bf16)
        upstream_ref[:, columns] = (act_grad * swish).astype(bf16)
        gate_grad = act_grad * up_part * sigma * (1.0 + gate_part * (1.0 - sigma))
        upstream_ref[:, gates] = gate_grad.astype(bf16)

    copies[2].start()
    copies[3].start()
    for piece in range(pieces):
        columns = slice(piece * depth, (piece + 1) * depth)
        second_ref[:, columns] = lax.dot_general(
            upstream_ref[...], w_ref[piece, :, : 2 * hidden], last, preferred_element_type=f32
        ).astype(bf16)
        shrunk_ref[:, columns] = lax.dot_general(
            active_ref[...], w_ref[piece, :, 2 * hidden :], last, preferred_element_type=f32
        ).astype(bf16)
    for copy in copies:
        copy.wait()


def hidden_pass(row, x_blocks, y_blocks, weights, length, wholes):
    width = weights[0].shape[0] * len(weights)
    count = sum(array.size for array, *_ in x_blocks) // width
    hidden = weights[0].shape[1] // 3
    kinds = [width, width, hidden, 2 * hidden]
    fresh = not wholes
    x_places, y_places = ([place for _, *place in blocks] for blocks in (x_blocks, y_blocks))
    given = len(x_blocks) + len(y_blocks) + len(weights)
    out = pl.pallas_call(
        lambda *refs: hidden_kernel(row, x_places, y_places, len(weights), fresh, *refs),
        out_shape=[jax.ShapeDtypeStruct((length, size), bf16) for size in kinds]
        + [jax.ShapeDtypeStruct((count, width), bf16)] * 2
        + [jax.ShapeDtypeStruct((8, 128), f32)],
        in_specs=anywhere(given + len(wholes)),
        out_specs=anywhere(4) + in_vmem(3),
        scratch_shapes=[pltpu.VMEM((count, size), bf16) for size in kinds]
        + [
            pltpu.VMEM((len(weights), *weights[0].shape), bf16),
            pltpu.VMEM((count, 3 * hidden), f32),
            pltpu.SemaphoreType.DMA((4,)),
            pltpu.SemaphoreType.DMA((len(weights),)),
            pltpu.SemaphoreType.DMA((len(x_blocks),)),
            pltpu.SemaphoreType.DMA((len(y_blocks),)),
        ],
        input_output_aliases={} if fresh else {given + i: i for i in range(4)},
        compiler_params=pltpu.CompilerParams(vmem_limit_bytes=KERNEL_VMEM),
        cost_estimate=brief,
        name="hidden",
    )(*[array for array, *_ in x_blocks + y_blocks], *weights, *wholes)
    return out[:4], out[4], out[5], out[6]


def attention_backward(queries, keys, values, up_blocks, weights, cosine, sine, places, blocks):
    length, own = queries.shape
    width = up_blocks[0][0].shape[1]
    heads = own // HEAD_DIM
    return pl.pallas_call(
        lambda *refs: backward_kernel([place for _, *place in up_blocks], len(weights), *refs),
        out_shape=[
            jax.ShapeDtypeStruct((length, width), bf16),
            jax.ShapeDtypeStruct((length, 3 * own), bf16),
        ]
        + [jax.ShapeDtypeStruct((end - start, width), bf16) for start, end in blocks]
        + [jax.ShapeDtypeStruct((8, 128), f32)],
        in_specs=in_vmem(3) + anywhere(len(up_blocks)) + in_vmem(6 + len(weights)),
        out_specs=in_vmem(3 + len(blocks)),
        scratch_shapes=[
            pltpu.VMEM((length, own), f32),
            pltpu.VMEM((length, own), f32),
            pltpu.SemaphoreType.DMA((len(up_blocks),)),
        ],
        compiler_params=pltpu.CompilerParams(vmem_limit_bytes=KERNEL_VMEM),
        cost_estimate=brief,
        name="attention_backward",
    )(
        queries,
        keys,
        values,
        *[array for array, *_ in up_blocks],
        *weights,
        cosine,
        sine,
        *places,
    )


def normed_rows(values):
    centered = values - jnp.mean(values, axis=-1, keepdims=True)
    inverse = lax.rsqrt(jnp.mean(centered * centered, axis=-1, keepdims=True) + norm_epsilon)
    return centered * inverse, inverse


def norm_back_rows(values, upstream):
    normed, inverse = normed_rows(values)
    return inverse * (
        upstream
        - jnp.mean(upstream, axis=-1, keepdims=True)
        - normed * jnp.mean(upstream * normed, axis=-1, keepdims=True)
    )


def row_call(kernel, name, kinds, *arrays, waits=()):
    shape = arrays[0].shape

    def run(*refs):
        refs[-1][...] = jnp.zeros_like(refs[-1])
        kernel(*refs[: len(arrays)], *refs[len(arrays) + len(waits) : -1])

    return pl.pallas_call(
        run,
        out_shape=[jax.ShapeDtypeStruct(shape, kind) for kind in kinds]
        + [jax.ShapeDtypeStruct((8, 128), f32)],
        in_specs=in_vmem(len(arrays)) + anywhere(len(waits)),
        out_specs=in_vmem(len(kinds) + 1),
        compiler_params=pltpu.CompilerParams(vmem_limit_bytes=KERNEL_VMEM),
        name=name,
    )(*arrays, *waits)


def wide(*refs):
    total = refs[0][...].astype(f32)
    for ref in refs[1:]:
        total = total + ref[...].astype(f32)
    return total


def join_kernel(token_ref, own_ref, up0, down0, up1, down1, residual_ref, norm_ref):
    middle = own_ref.shape[1] // 2
    for columns, refs in ((slice(0, middle), (up0, down0)), (slice(middle, None), (up1, down1))):
        residual_ref[:, columns] = token_ref[:, columns].astype(f32) + (
            own_ref[:, columns].astype(f32) + wide(*refs)
        )
    norm_ref[...] = normed_rows(residual_ref[...])[0].astype(bf16)


def turn_kernel(residual_ref, back_ref, own_ref, up0, down0, up1, down1, grad_ref, low_ref):
    upstream = own_ref[...].astype(f32) + jnp.concatenate([wide(up0, down0), wide(up1, down1)], 1)
    grad = back_ref[...].astype(f32) + norm_back_rows(residual_ref[...], upstream)
    grad_ref[...] = grad
    low_ref[...] = grad.astype(bf16)


def last_kernel(token_ref, grad_ref, residual_ref, own0, up0, down0, own1, up1, down1, in_ref, out_ref):
    in_ref[...] = grad_ref[...] + norm_back_rows(token_ref[...].astype(f32), wide(own0, up0, down0))
    out_ref[...] = (residual_ref[...] + wide(own1, up1, down1)).astype(bf16)


def weight_term(shards, k, products, adds=(), waits=(), cuts=1):
    length, width = products[0][0].shape
    depth = width // shards
    block = min(right.shape[1] for _, right in products)
    steps = [right.shape[1] // block for _, right in products]
    firsts = [sum(steps[:i]) for i in range(len(steps))]
    height = depth // cuts
    places = [(row, array.shape[0]) for array, row in adds]
    spans = places or [(i * height, height) for i in range(cuts)]

    def kernel(*refs):
        *outs, token = refs[-1 - cuts :]
        more = refs[2 * len(products) : 2 * len(products) + len(adds)]
        step = pl.program_id(0)
        token[...] = jnp.zeros_like(token)
        for index, first in enumerate(firsts):

            @pl.when((step >= first) & (step < first + steps[index]))
            def _():
                total = lax.dot_general(
                    refs[2 * index][...],
                    refs[2 * index + 1][...],
                    (((0,), (0,)), ((), ())),
                    preferred_element_type=f32,
                )
                for number, (row, rows) in enumerate(spans):
                    piece = total[row : row + rows]
                    if more:
                        piece = piece + more[number][...].astype(f32)
                    place = row % height
                    outs[row // height][place : place + rows, :] = piece.astype(bf16)

    specs, arrays = [], []
    for (left, right), first, size in zip(products, firsts, steps):
        specs.append(pl.BlockSpec((length, depth), lambda n: (0, k)))
        specs.append(
            pl.BlockSpec(
                (length, block),
                lambda n, first=first, size=size: (0, jnp.clip(n - first, 0, size - 1)),
            )
        )
        arrays += [left, right]
    return pl.pallas_call(
        kernel,
        grid=(sum(steps),),
        out_shape=[jax.ShapeDtypeStruct((height, sum(steps) * block), bf16)] * cuts
        + [jax.ShapeDtypeStruct((8, 128), f32)],
        in_specs=specs
        + [pl.BlockSpec((rows, block), lambda n: (0, n)) for _, rows in places]
        + anywhere(len(waits)),
        out_specs=[pl.BlockSpec((height, block), lambda n: (0, n))] * cuts
        + [pl.BlockSpec((8, 128), lambda n: (0, 0))],
        compiler_params=pltpu.CompilerParams(vmem_limit_bytes=KERNEL_VMEM),
        cost_estimate=brief,
        name="weight_term",
    )(*arrays, *[array for array, _ in adds], *waits)


def adam_kernel(rate, factor_ref, w_ref, m_ref, v_ref, g_ref, w_out, m_out, v_out):
    ranks, _, block = g_ref.shape
    for rank in range(ranks):
        columns = slice(rank * block, (rank + 1) * block)
        w_out[:, columns], m_out[:, columns], v_out[:, columns] = adam_update(
            w_ref[:, columns],
            m_ref[:, columns],
            v_ref[:, columns],
            g_ref[rank].astype(f32),
            factor_ref[0, 0],
            rate,
        )


def adam_step(weight, mean, square, grad, first, groups, factor, rate):
    ranks, rows, _ = grad.shape
    block = weight.shape[1] // (groups * ranks)
    held = max(1, min(ranks, ADAM_COLUMNS // block))
    steps = ranks // held
    flat = pl.BlockSpec((rows, held * block), lambda g, r: (0, g * steps + r))
    shape = jax.ShapeDtypeStruct(weight.shape, f32)
    return pl.pallas_call(
        lambda *refs: adam_kernel(rate, *refs),
        grid=(groups, steps),
        out_shape=[shape] * 3,
        in_specs=[
            pl.BlockSpec(memory_space=pltpu.SMEM),
            flat,
            flat,
            flat,
            pl.BlockSpec((held, rows, block), lambda g, r: (r, 0, first + g)),
        ],
        out_specs=[flat] * 3,
        compiler_params=pltpu.CompilerParams(vmem_limit_bytes=KERNEL_VMEM),
        cost_estimate=brief,
        name="adam_step",
    )(factor.reshape(1, 1), weight, mean, square, grad)


def body(ranks, shards):
    def run(
        tokens,
        cotangent,
        positions,
        segments,
        joint_weight,
        joint_mean,
        joint_square,
        output_weight,
        output_mean,
        output_square,
        expand_weight,
        expand_mean,
        expand_square,
        shrink_weight,
        shrink_mean,
        shrink_square,
    ):
        shard = lax.axis_index("fsdp")
        count, width = tokens.shape[1], tokens.shape[2]
        hidden = shrink_weight.shape[1]
        own = width // ranks
        own_hidden = hidden // ranks
        rows = width // (ranks * shards)
        y_rows = shards // CORES
        near_table = [
            [((f // CORES + k // CORES) % y_rows) * CORES + (f % CORES ^ k % CORES) for k in range(shards)]
            for f in range(shards)
        ]
        back_table = [[row.index(f) for f in range(shards)] for row in near_table]
        chunk_of = lax.dynamic_index_in_dim(jnp.array(near_table, jnp.int32), shard, 0, False)
        chunk_back = lax.dynamic_index_in_dim(jnp.array(back_table, jnp.int32), shard, 0, False)

        def to_inner(values):
            split = values.reshape(count, ranks, shards, rows).transpose(2, 0, 1, 3)
            return jnp.take(split, chunk_of, axis=0).transpose(1, 0, 2, 3).reshape(count, width)

        def to_outer(values):
            split = values.reshape(count, shards, ranks, rows).transpose(1, 0, 2, 3)
            return jnp.take(split, chunk_back, axis=0).transpose(1, 2, 0, 3).reshape(count, width)

        def columns_of(weight, groups):
            split = weight.astype(bf16).reshape(rows, groups, ranks, -1).transpose(2, 0, 1, 3)
            return split.reshape(ranks * rows, -1)

        def exchange(split):
            moved = lax.all_to_all(split.reshape(ranks, rows, -1), "ctx", 0, 0, tiled=True)
            return moved.reshape(ranks * rows, -1)

        def by_rank(moved):
            return moved.reshape(ranks, rows, -1)

        ahead, back = y_perm(shards, 1), y_perm(shards, -1)
        swap = core_perm(shards)

        def swapped(value):
            return lax.ppermute(value, "fsdp", swap)

        def across_y(block):
            blocks = [block]
            for _ in range(y_rows - 1):
                blocks.append(lax.ppermute(blocks[-1], "fsdp", back))
            return blocks

        def with_cores(blocks):
            return [piece for block in blocks for piece in (block, swapped(block))]

        token_low = to_inner(tokens[0])
        back_low = to_inner(cotangent[0])
        joint_split = columns_of(joint_weight, 3)
        output_split = columns_of(output_weight, 1)
        near_moved = exchange(jnp.concatenate([joint_split, output_split], 1))
        far_split = jnp.concatenate([columns_of(expand_weight, 2), columns_of(shrink_weight, 1)], 1)
        near_moved, far_split = hold(near_moved, far_split)
        far_moved = exchange(far_split)
        near_blocks = across_y(near_moved)

        order = ring_order(ranks)
        block_table = [
            [order[(order.index(i) + d) % ranks] for d in pair_order(ranks)] for i in range(ranks)
        ]
        block_of = lax.dynamic_index_in_dim(
            jnp.array(block_table, jnp.int32), lax.axis_index("ctx"), 0, False
        )
        pos = jnp.take(positions[0].reshape(ranks, count), block_of, axis=0).reshape(-1)
        seg = jnp.take(segments[0].reshape(ranks, count), block_of, axis=0).reshape(-1)
        places = (pos[:, None], seg[:, None], pos[None, :], seg[None, :])
        turn = HEAD_DIM // 2
        inverse = jnp.exp(jnp.arange(turn).astype(f32) * (-2.0 * math.log(rope_base) / HEAD_DIM))
        angles = pos.astype(f32)[:, None] * inverse[None, :]
        cosine, sine = jnp.cos(angles), jnp.sin(angles)
        cosine = jnp.concatenate([cosine, cosine], 1)
        sine = jnp.concatenate([-sine, sine], 1)

        def collect(products):
            total = None
            waits = yield
            for step in range(y_rows - 1, -1, -1):
                *terms, token = weight_term(shards, step * CORES + 1, products, (), waits, 4)
                adds = [(swapped(term), i * term.shape[0]) for i, term in enumerate(terms)]
                waits = yield token
                term, token = weight_term(shards, step * CORES, products, adds, waits)
                if step == 0:
                    yield token
                if total is not None:
                    term = (term.astype(f32) + total.astype(f32)).astype(bf16)
                if step:
                    total = lax.ppermute(term, "fsdp", ahead)
                    waits = yield token
            yield term

        def finish(work):
            result = None
            while True:
                try:
                    result = work.send([])
                except StopIteration:
                    return result

        def collect_all(products):
            work = collect(products)
            next(work)
            return finish(work)

        def square_sum(grad):
            return jnp.sum(jnp.square(grad.astype(f32)))

        first_own = layer_norm(token_low.astype(f32)).astype(bf16)
        first_own, far_moved, back_low, *near_blocks[1:] = hold(
            first_own, far_moved, back_low, *near_blocks[1:]
        )
        near = with_cores(near_blocks)
        far_blocks = across_y(far_moved)
        first_blocks = ring_gather(first_own, ranks, 2)
        near_core = swapped(far_moved)
        first_blocks, (back_low, near_core) = hold_ends(first_blocks, back_low, near_core)
        blocks = block_rows(ranks, count)
        work = attention_forward(flat(first_blocks), near, cosine, sine, places, blocks)
        back_blocks = ring_gather(
            back_low, ranks, beside=lambda step: next(work) if step <= 3 else []
        )
        first_norm, queries, keys, values, attended, branch = list(work)[-1]
        middle = width // 2
        branch_sides = (branch, 0, middle), (branch, middle, width)
        sends = first_sends(*branch_sides)
        back_blocks, held = hold_ends(back_blocks, *sends, *far_blocks[1:])
        sends, far_blocks[1:] = held[:4], held[4:]
        cores = [near_core] + [swapped(block) for block in far_blocks[1:]]
        far = [piece for pair in zip(far_blocks, cores) for piece in pair]
        sums = twin_scatter(
            *branch_sides, sends, ranks, lambda turn, _: cores[1:] if turn == 2 else []
        )
        residual, second_own, _ = row_call(
            join_kernel, "join", (f32, bf16), token_low, branch[0], *sums[0], *sums[1]
        )

        half = ranks // 2
        length = ranks * count
        wholes, terms, shrunk = [], [None] * (half + 1), [None] * (half + 1)

        def pass_rows(step, x_blocks, y_blocks):
            first = x_blocks[0][1] if step < half else 0
            far_row = (ranks - 1) * count

            def local(given):
                return [
                    (array, count if step == half and row == far_row else row - first, column)
                    for array, row, column in given
                ]

            start = 2 * (step - 1) * count
            wholes[:], second, out, mark = hidden_pass(
                start, local(x_blocks), local(y_blocks), far, length, list(wholes)
            )
            if step < half:
                terms[step], shrunk[step] = second, out
            else:
                terms[0], terms[half] = second[:count], second[count:]
                shrunk[0], shrunk[half] = out[:count], out[count:]
            return [mark]

        def arrived(step, x_blocks):
            return pass_rows(step, x_blocks, back_blocks[step % half])

        ring_gather(second_own, ranks, 1, arrived)
        second_norm, back_rows, activated, upstream = wholes
        shrink_work = collect([(back_rows, activated)])
        expand_work = collect([(second_norm, upstream)])
        next(shrink_work), next(expand_work)

        def first_half(turn, tokens):
            return [shrink_work.send([tokens[turn - 2]])] if turn in (2, 4) and y_rows > 1 else []

        term_sides = (terms, 0, middle), (terms, middle, width)
        sums = twin_scatter(*term_sides, first_sends(*term_sides), ranks, first_half)
        residual_grad, branch_low, mark = row_call(
            turn_kernel, "turn", (f32, bf16), residual, back_low, terms[0], *sums[0], *sums[1]
        )

        def second_half(step):
            if y_rows == 1 or step > 3:
                return []
            work = [expand_work, shrink_work] if step == 3 else [expand_work]
            return [one.send([mark]) for one in work]

        branch_blocks = ring_gather(branch_low, ranks, beside=second_half)
        branch_blocks, (shrink_grad, _) = hold_ends(
            branch_blocks, finish(shrink_work), expand_work.send([])
        )
        shrink_back = exchange(shrink_grad)
        branch_grad, joint_upstream, *first_part, mark = attention_backward(
            queries, keys, values, flat(branch_blocks), near, cosine, sine, places, blocks
        )
        expand_grad, shrink_back, _ = hold(finish(expand_work), shrink_back, mark)
        expand_back = exchange(expand_grad)
        near_grad = collect_all([(first_norm, joint_upstream), (branch_grad, attended)])
        near_grad, expand_back = hold(near_grad, expand_back)
        near_back = exchange(near_grad)
        squares = square_sum(near_back) + square_sum(shrink_back) + square_sum(expand_back)
        total = sum_everywhere(squares, ranks, shards)
        last_sides = (first_part, 0, width), (shrunk, 0, width)
        *sends, near_back = hold(*first_sends(*last_sides), near_back)
        grad_norm = jnp.sqrt(total[0, 0])
        factor = jnp.minimum(1.0, clip_limit / (grad_norm + 1e-06))
        joint_new = adam_step(
            joint_weight, joint_mean, joint_square, by_rank(near_back), 0, 3, factor, main_rate
        )
        output_new = adam_step(
            output_weight, output_mean, output_square, by_rank(near_back), 3, 1, factor, output_rate
        )
        expand_new = adam_step(
            expand_weight, expand_mean, expand_square, by_rank(expand_back), 0, 2, factor, main_rate
        )
        shrink_new = adam_step(
            shrink_weight, shrink_mean, shrink_square, by_rank(shrink_back), 0, 1, factor, main_rate
        )
        sums = twin_scatter(
            *last_sides,
            sends,
            ranks,
            lambda turn, _: {0: [total], 2: joint_new + output_new, 3: shrink_new}.get(turn, []),
        )
        input_inner, layer_inner, _ = row_call(
            last_kernel,
            "last",
            (f32, bf16),
            token_low,
            residual_grad,
            residual,
            first_part[0],
            *sums[0],
            shrunk[0],
            *sums[1],
            waits=expand_new[:1],
        )
        input_grad = to_outer(input_inner)[None]
        layer_output = to_outer(layer_inner)[None]
        return (
            layer_output,
            input_grad,
            grad_norm,
            *joint_new,
            *output_new,
            *expand_new,
            *shrink_new,
        )

    return run


def solution(mesh):
    tokens_spec = P("fsdp", "ctx", None)
    place_spec = P("fsdp", None)
    weight_spec = P(("ctx", "fsdp"), None)
    return jax.shard_map(
        body(mesh.shape["ctx"], mesh.shape["fsdp"]),
        mesh=mesh,
        in_specs=(tokens_spec, tokens_spec, place_spec, place_spec) + (weight_spec,) * 12,
        out_specs=(tokens_spec, tokens_spec, P()) + (weight_spec,) * 12,
        check_vma=False,
    )
```
